32 devices in a mesh: wide: 8 (over y, x, core), narrow: 4 (over z).
Axes of the slice: x: 2, y: 2, z: 4, core: 2. Of those that a mesh axis runs over, the one named last changes fastest.
Arguments:
- stream: bfloat16 [128, 128, 768], P(('wide', 'narrow')), may hold values from -6 to 6
- cotangent: bfloat16 [128, 128, 768], P(('wide', 'narrow')), may hold values from -6 to 6
- segment_ids: int32 [128, 128], P(('wide', 'narrow')), may hold values from 0 to 2, as said below
- first_gain: bfloat16 [768], P(('wide', 'narrow')), may hold values from 0.099609375 to 1.8984375
- first_shift: bfloat16 [768], P(('wide', 'narrow')), may hold values from -1.25 to 1.25
- first_packed: bfloat16 [768, 2304], P(('wide', 'narrow')), may hold values from -0.21875 to 0.21875
- first_lift: bfloat16 [2304], P(('wide', 'narrow')), may hold values from -1.25 to 1.25
- first_blend: bfloat16 [768, 768], P(('wide', 'narrow')), may hold values from -1.25 to 1.25
- first_nudge: bfloat16 [768], P(('wide', 'narrow')), may hold values from -1.25 to 1.25
- first_scale: bfloat16 [768], P(('wide', 'narrow')), may hold values from 0.099609375 to 1.8984375
- first_center: bfloat16 [768], P(('wide', 'narrow')), may hold values from -1.25 to 1.25
- first_widen: bfloat16 [768, 3072], P(('wide', 'narrow')), may hold values from -0.21875 to 0.21875
- first_boost: bfloat16 [3072], P(('wide', 'narrow')), may hold values from -1.25 to 1.25
- first_shrink: bfloat16 [3072, 768], P(('wide', 'narrow')), may hold values from -0.109375 to 0.109375
- first_settle: bfloat16 [768], P(('wide', 'narrow')), may hold values from -1.25 to 1.25
- second_gain: bfloat16 [768], P(('wide', 'narrow')), may hold values from 0.099609375 to 1.8984375
- second_shift: bfloat16 [768], P(('wide', 'narrow')), may hold values from -1.25 to 1.25
- second_packed: bfloat16 [768, 2304], P(('wide', 'narrow')), may hold values from -0.21875 to 0.21875
- second_lift: bfloat16 [2304], P(('wide', 'narrow')), may hold values from -1.25 to 1.25
- second_blend: bfloat16 [768, 768], P(('wide', 'narrow')), may hold values from -1.25 to 1.25
- second_nudge: bfloat16 [768], P(('wide', 'narrow')), may hold values from -1.25 to 1.25
- second_scale: bfloat16 [768], P(('wide', 'narrow')), may hold values from 0.099609375 to 1.8984375
- second_center: bfloat16 [768], P(('wide', 'narrow')), may hold values from -1.25 to 1.25
- second_widen: bfloat16 [768, 3072], P(('wide', 'narrow')), may hold values from -0.21875 to 0.21875
- second_boost: bfloat16 [3072], P(('wide', 'narrow')), may hold values from -1.25 to 1.25
- second_shrink: bfloat16 [3072, 768], P(('wide', 'narrow')), may hold values from -0.109375 to 0.109375
- second_settle: bfloat16 [768], P(('wide', 'narrow')), may hold values from -1.25 to 1.25
Outputs:
- result: bfloat16 [128, 128, 768], P(('wide', 'narrow'))
- stream_grad: float32 [128, 128, 768], P(('wide', 'narrow'))
- firstgrad_gain: float32 [768], P(('wide', 'narrow'))
- firstgrad_shift: float32 [768], P(('wide', 'narrow'))
- firstgrad_packed: float32 [768, 2304], P(('wide', 'narrow'))
- firstgrad_lift: float32 [2304], P(('wide', 'narrow'))
- firstgrad_blend: float32 [768, 768], P(('wide', 'narrow'))
- firstgrad_nudge: float32 [768], P(('wide', 'narrow'))
- firstgrad_scale: float32 [768], P(('wide', 'narrow'))
- firstgrad_center: float32 [768], P(('wide', 'narrow'))
- firstgrad_widen: float32 [768, 3072], P(('wide', 'narrow'))
- firstgrad_boost: float32 [3072], P(('wide', 'narrow'))
- firstgrad_shrink: float32 [3072, 768], P(('wide', 'narrow'))
- firstgrad_settle: float32 [768], P(('wide', 'narrow'))
- secondgrad_gain: float32 [768], P(('wide', 'narrow'))
- secondgrad_shift: float32 [768], P(('wide', 'narrow'))
- secondgrad_packed: float32 [768, 2304], P(('wide', 'narrow'))
- secondgrad_lift: float32 [2304], P(('wide', 'narrow'))
- secondgrad_blend: float32 [768, 768], P(('wide', 'narrow'))
- secondgrad_nudge: float32 [768], P(('wide', 'narrow'))
- secondgrad_scale: float32 [768], P(('wide', 'narrow'))
- secondgrad_center: float32 [768], P(('wide', 'narrow'))
- secondgrad_widen: float32 [768, 3072], P(('wide', 'narrow'))
- secondgrad_boost: float32 [3072], P(('wide', 'narrow'))
- secondgrad_shrink: float32 [3072, 768], P(('wide', 'narrow'))
- secondgrad_settle: float32 [768], P(('wide', 'narrow'))
The draws below stay inside these ranges and needn't reach their ends.
Inputs may be any that keep to these rules, and one draw needn't show every extreme that they name: `segment_ids`: along each row of 128 positions the ids start at 0 and never fall; each row holds two or three segments, and row 0 holds three.
All inputs are finite; a program needn't handle non-finite values.
Results may differ from the reference program's by a relative error of at most 0.018.
Values may be sent and summed in bfloat16 or wider, within the bound.
No kernel may reach another device: no remote copies, remote signals or barrier semaphores. Data moves between devices by JAX's collectives and lax.ppermute only.
A program may use at most 256 MiB of HBM per device.

```python
import math
import jax
import jax.numpy as jnp
from jax import lax

D = 768
HEADS = 12
HEAD_DIM = 64
ROT = 16
FF = 3072
SEQ = 128
ROWS = 128


def draw_segment_ids(key, part):
    key = jax.random.fold_in(key, 11)
    key_one, key_two, key_three = jax.random.split(key, 3)
    lowest = max(1, SEQ // 5)
    highest = SEQ // 2
    first_len = jax.random.randint(key_one, (ROWS, 1), lowest, highest)
    second_len = jax.random.randint(key_two, (ROWS, 1), lowest, highest)
    third_on = jax.random.randint(key_three, (ROWS, 1), 0, 2)
    third_on = jnp.where(jnp.arange(ROWS)[:, None] == 0, 1, third_on)
    place = jnp.arange(SEQ)[None, :]
    return ((place >= first_len).astype(jnp.int32) + third_on * (place >= first_len + second_len).astype(jnp.int32)).astype(jnp.int32)


def block_levels(key, dims, pieces, smallest, high):
    loudness = 1.0
    for axis_at, blocks in pieces:
        draws = jax.random.uniform(jax.random.fold_in(jax.random.fold_in(key, 6), axis_at), (blocks,), jnp.float32, smallest / len(pieces), high / len(pieces))
        loudness = loudness * jnp.repeat(jnp.exp(draws), dims[axis_at] // blocks).reshape((-1,) + (1,) * (len(dims) - 1 - axis_at))
    return loudness


def bell_draw(rng, shape, deviation, bound, cuts=(), kind=jnp.bfloat16):
    drawn = jax.random.normal(rng, shape, jnp.float32) * deviation
    if len(cuts) > 0:
        drawn = block_levels(rng, shape, cuts, -0.22, 0.18) * drawn
    return jnp.clip(drawn, min=-bound, max=bound).astype(kind)


def setup_inputs(seed: int = 0) -> dict:
    key_of = jax.random.split(jax.random.key(seed), 28)
    stream = bell_draw(key_of[0], (ROWS, SEQ, D), 1.0, 6.0, ((0, 32),))
    cotangent = bell_draw(key_of[1], (ROWS, SEQ, D), 1.0, 6.0, ((0, 32),))
    segment_ids = draw_segment_ids(jax.random.fold_in(key_of[27], 71), 0)
    first_gain = jnp.clip(1.0 + 0.18 * jax.random.normal(key_of[3], (D,), jnp.float32), 0.099609375, 1.8984375).astype(jnp.bfloat16)
    first_shift = bell_draw(key_of[4], (D,), 0.2, 1.25, ((0, 32),))
    first_packed = bell_draw(key_of[5], (D, 3 * D), D ** -0.5, 0.21875, ((0, 32),))
    first_lift = bell_draw(key_of[6], (3 * D,), 0.2, 1.25, ((0, 32),))
    first_blend = bell_draw(key_of[7], (D, D), (D // 32) ** -0.5, 1.25, ((0, 32),))
    first_nudge = bell_draw(key_of[8], (D,), 0.2, 1.25, ((0, 32),))
    first_scale = jnp.clip(1.0 + 0.18 * jax.random.normal(key_of[9], (D,), jnp.float32), 0.099609375, 1.8984375).astype(jnp.bfloat16)
    first_center = bell_draw(key_of[10], (D,), 0.2, 1.25, ((0, 32),))
    first_widen = bell_draw(key_of[11], (D, FF), D ** -0.5, 0.21875, ((0, 32),))
    first_boost = bell_draw(key_of[12], (FF,), 0.2, 1.25, ((0, 32),))
    first_shrink = bell_draw(key_of[13], (FF, D), FF ** -0.5, 0.109375, ((0, 32),))
    first_settle = bell_draw(key_of[14], (D,), 0.2, 1.25, ((0, 32),))
    second_gain = jnp.clip(1.0 + 0.18 * jax.random.normal(key_of[15], (D,), jnp.float32), 0.099609375, 1.8984375).astype(jnp.bfloat16)
    second_shift = bell_draw(key_of[16], (D,), 0.2, 1.25, ((0, 32),))
    second_packed = bell_draw(key_of[17], (D, 3 * D), D ** -0.5, 0.21875, ((0, 32),))
    second_lift = bell_draw(key_of[18], (3 * D,), 0.2, 1.25, ((0, 32),))
    second_blend = bell_draw(key_of[19], (D, D), (D // 32) ** -0.5, 1.25, ((0, 32),))
    second_nudge = bell_draw(key_of[20], (D,), 0.2, 1.25, ((0, 32),))
    second_scale = jnp.clip(1.0 + 0.18 * jax.random.normal(key_of[21], (D,), jnp.float32), 0.099609375, 1.8984375).astype(jnp.bfloat16)
    second_center = bell_draw(key_of[22], (D,), 0.2, 1.25, ((0, 32),))
    second_widen = bell_draw(key_of[23], (D, FF), D ** -0.5, 0.21875, ((0, 32),))
    second_boost = bell_draw(key_of[24], (FF,), 0.2, 1.25, ((0, 32),))
    second_shrink = bell_draw(key_of[25], (FF, D), FF ** -0.5, 0.109375, ((0, 32),))
    second_settle = bell_draw(key_of[26], (D,), 0.2, 1.25, ((0, 32),))
    return dict(stream=stream, cotangent=cotangent, segment_ids=segment_ids, first_gain=first_gain, first_shift=first_shift, first_packed=first_packed, first_lift=first_lift, first_blend=first_blend, first_nudge=first_nudge, first_scale=first_scale, first_center=first_center, first_widen=first_widen, first_boost=first_boost, first_shrink=first_shrink, first_settle=first_settle, second_gain=second_gain, second_shift=second_shift, second_packed=second_packed, second_lift=second_lift, second_blend=second_blend, second_nudge=second_nudge, second_scale=second_scale, second_center=second_center, second_widen=second_widen, second_boost=second_boost, second_shrink=second_shrink, second_settle=second_settle)


EPS = 1e-05

@jax.custom_vjp
def low(v):
    return lax.optimization_barrier(v.astype(jnp.bfloat16)).astype(jnp.float32)

@jax.custom_vjp
def low_back(v):
    return v

def low_keep(v):
    return (low(v), None)

def low_pass(kept, grad):
    return (grad,)

def back_keep(v):
    return (v, None)

def back_low(kept, grad):
    return (low(grad),)
low.defvjp(low_keep, low_pass)
low_back.defvjp(back_keep, back_low)

def geometry(segments):
    length = segments.shape[-1]
    before = lax.optimization_barrier(jnp.sum((segments[:, None, :] < segments[:, :, None]).astype(jnp.int32), -1))
    place = jnp.arange(length, dtype=jnp.int32)
    position = (place[None, :] - before).astype(jnp.float32)
    freqs = 10000.0 ** (-(jnp.arange(ROT // 2, dtype=jnp.float32) * 2.0 / ROT))
    angle = position[:, :, None] * freqs[None, None, :]
    angle = jnp.concatenate([angle, angle], -1)[:, :, None, :]
    allowed = (segments[:, :, None] == segments[:, None, :]) & (place[:, None] >= place[None, :])[None]
    return (jnp.cos(angle), jnp.sin(angle), allowed)

def normalize(values, gain, shift):
    centered = values - lax.optimization_barrier(jnp.mean(values, -1, keepdims=True))
    spread = lax.optimization_barrier(jnp.mean(centered * centered, -1, keepdims=True))
    return centered * lax.rsqrt(spread + EPS) * gain + shift

def rotate(block, cosine, sine):
    half = ROT // 2
    front = block[..., :ROT]
    turned = jnp.concatenate([-front[..., half:], front[..., :half]], -1)
    return jnp.concatenate([front * cosine + turned * sine, block[..., ROT:]], -1)

def matmul(left, right):
    return jnp.dot(left, right, precision=lax.Precision.HIGHEST)

def layer(inputs, weights, cosine, sine, allowed):
    gain, shift, packed, lift, blend, nudge, scale, center, widen, boost, shrink, settle = weights
    count, length, width = inputs.shape
    factor = HEAD_DIM ** (-0.5)
    flat = inputs.reshape(count * length, width)
    first = low(normalize(flat, gain, shift))
    mixed = low_back(matmul(first, packed) + lift)
    heads = mixed.reshape(count, length, 3, HEADS, HEAD_DIM)
    query = low(rotate(heads[:, :, 0], cosine, sine))
    keys = low(rotate(heads[:, :, 1], cosine, sine))
    values = low(heads[:, :, 2])
    raw = low_back(jnp.einsum('rqhd,rkhd->rhqk', query, keys, precision=lax.Precision.HIGHEST))
    logits = jnp.where(allowed[:, None], raw * factor, -1000000000.0)
    probs = low(jax.nn.softmax(logits, -1))
    attended = jnp.einsum('rhqk,rkhd->rqhd', probs, values, precision=lax.Precision.HIGHEST)
    attended = low(low_back(attended)).reshape(count * length, width)
    att_out = low_back(matmul(attended, blend) + nudge)
    second = low(normalize(flat, scale, center))
    upward = low_back(matmul(second, widen) + boost)
    active = low(jax.nn.gelu(upward, approximate=False))
    mlp_out = low_back(matmul(active, shrink) + settle)
    return (flat + att_out + mlp_out).reshape(count, length, width)

def reference(stream, cotangent, segment_ids, first_gain, first_shift, first_packed, first_lift, first_blend, first_nudge, first_scale, first_center, first_widen, first_boost, first_shrink, first_settle, second_gain, second_shift, second_packed, second_lift, second_blend, second_nudge, second_scale, second_center, second_widen, second_boost, second_shrink, second_settle):
    weights = tuple((item.astype(jnp.float32) for item in (first_gain, first_shift, first_packed, first_lift, first_blend, first_nudge, first_scale, first_center, first_widen, first_boost, first_shrink, first_settle, second_gain, second_shift, second_packed, second_lift, second_blend, second_nudge, second_scale, second_center, second_widen, second_boost, second_shrink, second_settle)))
    group = math.gcd(ROWS, 32)
    blocks = ROWS // group
    segment_blocks = segment_ids.reshape(blocks, group, SEQ)

    def forward(inputs, params):

        def one_block(pair):
            block, segments = pair
            cosine, sine, allowed = geometry(segments)
            middle = layer(block, params[:12], cosine, sine, allowed)
            return layer(middle, params[12:], cosine, sine, allowed)
        outputs = lax.map(jax.checkpoint(one_block), (inputs.reshape(blocks, group, SEQ, D), segment_blocks))
        return outputs.reshape(ROWS, SEQ, D)
    outputs, pullback = jax.vjp(forward, stream.astype(jnp.float32), weights)
    grad_in, grads = pullback(cotangent.astype(jnp.float32))
    return (outputs.astype(jnp.bfloat16), grad_in, grads[0], grads[1], grads[2], grads[3], grads[4], grads[5], grads[6], grads[7], grads[8], grads[9], grads[10], grads[11], grads[12], grads[13], grads[14], grads[15], grads[16], grads[17], grads[18], grads[19], grads[20], grads[21], grads[22], grads[23])
```

```python
import functools
import jax
import jax.numpy as jnp
from jax import lax
from jax.sharding import PartitionSpec as P
from jax.experimental import pallas as pl
from jax.experimental.pallas import tpu as pltpu

HEADS = 12
ROT = 16
EPS = 1e-05
F32 = jnp.float32
BF16 = jnp.bfloat16
LANES = 128
MASKED = -1000000000.0
VMEM_LIMIT = 24 * 1024 * 1024


def params(**more):
    return pltpu.CompilerParams(vmem_limit_bytes=VMEM_LIMIT, **more)


def launch(body, operands, out_shape, after=(), in_specs=None, flops=0, moved=4_000_000, **more):
    count = len(operands)
    if in_specs is None:
        in_specs = [pl.BlockSpec(memory_space=pltpu.VMEM)] * count

    def kernel(*refs):
        body(*refs[:count], *refs[count + len(after) :])

    return pl.pallas_call(
        kernel,
        out_shape=out_shape,
        in_specs=list(in_specs) + [pl.BlockSpec(memory_space=pl.ANY)] * len(after),
        compiler_params=params(),
        cost_estimate=pl.CostEstimate(flops=0, bytes_accessed=0, transcendentals=0),
        **more,
    )(*operands, *after)


def like(shape, kind):
    return jax.ShapeDtypeStruct(tuple(shape), kind)


def dot(left, right):
    return lax.dot_general(left, right, (((1,), (0,)), ((), ())), preferred_element_type=F32)


def dot_nt(left, right):
    return lax.dot_general(left, right, (((1,), (1,)), ((), ())), preferred_element_type=F32)


def dot_tn(left, right):
    return lax.dot_general(left, right, (((0,), (0,)), ((), ())), preferred_element_type=F32)


def tables(segments, head_size):
    length = segments.shape[-1]
    before = jnp.sum((segments[:, None, :] < segments[:, :, None]).astype(jnp.int32), -1)
    place = jnp.arange(length, dtype=jnp.int32)
    position = (place[None, :] - before).astype(F32).reshape(-1, 1)
    half = ROT // 2
    lane = jnp.arange(LANES, dtype=jnp.int32) % head_size
    freqs = 10000.0 ** (-((lane % half).astype(F32) * 2.0 / ROT))
    angle = position * freqs[None, :]
    lane = lane[None, :]
    cosine = jnp.where(lane < ROT, jnp.cos(angle), 1.0)
    sine = jnp.sin(angle)
    low = jnp.where(lane < half, -sine, 0.0)
    high = jnp.where((lane >= half) & (lane < ROT), sine, 0.0)
    allowed = (segments[:, :, None] == segments[:, None, :]) & (place[:, None] >= place[None, :])[
        None
    ]
    return cosine, low, high, jnp.where(allowed, 0.0, -1.0).astype(F32)


def whiten(x):
    centered = x - jnp.mean(x, -1, keepdims=True)
    spread = jnp.mean(centered * centered, -1, keepdims=True)
    scale = lax.rsqrt(spread + EPS)
    return centered * scale, scale


def lane_masks(head_size, value):
    lane = lax.broadcasted_iota(jnp.int32, (1, LANES), 1)
    return [
        jnp.where((lane >= i * head_size) & (lane < (i + 1) * head_size), value, 0.0).astype(BF16)
        for i in range(LANES // head_size)
    ]


def stacked(block, masks):
    return jnp.concatenate([block * m for m in masks], 0)


def softmax_halves(scores, masked):
    out = []
    for i in range(scores.shape[1] // LANES):
        logits = jnp.where(masked, MASKED, scores[:, i * LANES : (i + 1) * LANES])
        expo = jnp.exp(logits - jnp.max(logits, -1, keepdims=True))
        out.append(expo * (1.0 / jnp.sum(expo, -1, keepdims=True)))
    return out


def attention_forward(
    h_ref, gain_ref, shift_ref, packed_ref, lift_ref, cos_ref, low_ref, high_ref, mask_ref,
    blend_ref, nudge_ref,
    first_t_ref, q_ref, k_ref, v_ref, att_t_ref, base_ref,
    first_ref, att_ref,
):
    rows, length, _ = mask_ref.shape
    width = h_ref.shape[1]
    head_size = width // HEADS

    @pl.loop(0, rows)
    def _(r):
        at = pl.ds(pl.multiple_of(r * length, length), length)
        normed, _ = whiten(h_ref[at, :].astype(F32))
        first = (normed * gain_ref[...].astype(F32) + shift_ref[...].astype(F32)).astype(BF16)
        first_ref[at, :] = first
        first_t_ref[:, at] = first.T

    tile = 2 * LANES
    for j in range(width // tile):
        for part, out_ref in enumerate((q_ref, k_ref, v_ref)):
            cols = slice(part * width + j * tile, part * width + (j + 1) * tile)
            mixed = dot(first_ref[...], packed_ref[:, cols]) + lift_ref[:, cols].astype(F32)
            for b in range(tile // LANES):
                block = mixed[:, b * LANES : (b + 1) * LANES]
                if part < 2:
                    block = (
                        block * cos_ref[...]
                        + pltpu.roll(block, LANES - ROT // 2, 1) * low_ref[...]
                        + pltpu.roll(block, ROT // 2, 1) * high_ref[...]
                    )
                out_ref[:, j * tile + b * LANES : j * tile + (b + 1) * LANES] = block.astype(BF16)

    scaled = lane_masks(head_size, head_size ** (-0.5))
    plain = lane_masks(head_size, 1.0)

    @pl.loop(0, rows)
    def _(r):
        at = pl.ds(pl.multiple_of(r * length, length), length)
        masked = mask_ref[r] < 0.0
        for p in range(width // LANES):
            cols = slice(p * LANES, (p + 1) * LANES)
            scores = dot_nt(q_ref[at, cols], stacked(k_ref[at, cols], scaled))
            probs = jnp.concatenate([p.astype(BF16) for p in softmax_halves(scores, masked)], 1)
            attended = dot(probs, stacked(v_ref[at, cols], plain)).astype(BF16)
            att_ref[at, cols] = attended
            att_t_ref[cols, at] = attended.T

    for j in range(width // tile):
        cols = slice(j * tile, (j + 1) * tile)
        base_ref[:, cols] = (
            h_ref[:, cols].astype(F32)
            + dot(att_ref[...], blend_ref[:, cols])
            + nudge_ref[:, cols].astype(F32)
        )


def run_attention_forward(h, gain, shift, packed, lift, turns, blend, nudge, after):
    tokens, width = h.shape
    return launch(
        attention_forward,
        (h, gain, shift, packed, lift, *turns, blend, nudge),
        (
            like((width, tokens), BF16),
            like((tokens, width), BF16),
            like((tokens, width), BF16),
            like((tokens, width), BF16),
            like((width, tokens), BF16),
            like((tokens, width), F32),
        ),
        after,
        flops=8 * tokens * width * width,
        moved=40_000_000,
        scratch_shapes=[pltpu.VMEM((tokens, width), BF16), pltpu.VMEM((tokens, width), BF16)],
        name="attention_forward",
    )


def gelu_pair(u):
    z = jnp.abs(u) * 0.7071067811865476
    t = 1.0 / (1.0 + 0.3275911 * z)
    poly = t * (
        0.127414796
        + t * (-0.142248368 + t * (0.7107068705 + t * (-0.7265760135 + t * 0.5307027145)))
    )
    bell = jnp.exp(-0.5 * u * u)
    tail = poly * bell
    cdf = jnp.where(u < 0.0, tail, 1.0 - tail)
    return u * cdf, cdf + u * bell * 0.3989422804014327


def mlp_forward(
    h_ref, scale_ref, center_ref, widen_ref, boost_ref, shrink_ref, settle_ref, base_ref,
    second_t_ref, active_t_ref, slope_ref, out_ref,
    second_ref,
):
    step = pl.program_id(0)
    length = LANES
    rows = h_ref.shape[0] // length

    @pl.when(step == 0)
    def _():
        @pl.loop(0, rows)
        def _(r):
            at = pl.ds(pl.multiple_of(r * length, length), length)
            normed, _ = whiten(h_ref[at, :].astype(F32))
            second = (normed * scale_ref[...].astype(F32) + center_ref[...].astype(F32)).astype(BF16)
            second_ref[at, :] = second
            second_t_ref[:, at] = second.T
        out_ref[...] = base_ref[...] + settle_ref[...].astype(F32)

    upward = dot(second_ref[...], widen_ref[...]) + boost_ref[...].astype(F32)
    active, slope = gelu_pair(upward)
    active = active.astype(BF16)
    slope_ref[...] = slope.astype(BF16)
    active_t_ref[...] = active.T
    out_ref[...] += dot(active, shrink_ref[...])


def run_mlp_forward(h, scale, center, widen, boost, shrink, settle, base, after, tile=512):
    tokens, width = h.shape
    hidden = widen.shape[1]
    whole = lambda shape: pl.BlockSpec(shape, lambda j: (0, 0))
    return launch(
        mlp_forward,
        (h, scale, center, widen, boost, shrink, settle, base),
        (
            like((width, tokens), BF16),
            like((hidden, tokens), BF16),
            like((tokens, hidden), BF16),
            like((tokens, width), F32),
        ),
        after,
        grid=(hidden // tile,),
        in_specs=[
            whole((tokens, width)),
            whole((1, width)),
            whole((1, width)),
            pl.BlockSpec((width, tile), lambda j: (0, j)),
            pl.BlockSpec((1, tile), lambda j: (0, j)),
            pl.BlockSpec((tile, width), lambda j: (j, 0)),
            whole((1, width)),
            whole((tokens, width)),
        ],
        out_specs=(
            whole((width, tokens)),
            pl.BlockSpec((tile, tokens), lambda j: (j, 0)),
            pl.BlockSpec((tokens, tile), lambda j: (0, j)),
            whole((tokens, width)),
        ),
        flops=4 * tokens * width * hidden,
        moved=50_000_000,
        scratch_shapes=[pltpu.VMEM((tokens, width), BF16)],
        name="mlp_forward",
    )


def mlp_up(
    h_ref, scale_ref, center_ref, widen_ref, boost_ref,
    second_t_ref, active_t_ref, slope_ref,
    second_ref,
):
    step = pl.program_id(0)
    length = LANES
    rows = h_ref.shape[0] // length

    @pl.when(step == 0)
    def _():
        @pl.loop(0, rows)
        def _(r):
            at = pl.ds(pl.multiple_of(r * length, length), length)
            normed, _ = whiten(h_ref[at, :].astype(F32))
            second = (normed * scale_ref[...].astype(F32) + center_ref[...].astype(F32)).astype(BF16)
            second_ref[at, :] = second
            second_t_ref[:, at] = second.T

    upward = dot(second_ref[...], widen_ref[...]) + boost_ref[...].astype(F32)
    active, slope = gelu_pair(upward)
    slope_ref[...] = slope.astype(BF16)
    active_t_ref[...] = active.astype(BF16).T


def run_mlp_up(h, scale, center, widen, boost, after, tile=512):
    tokens, width = h.shape
    hidden = widen.shape[1]
    whole = lambda shape: pl.BlockSpec(shape, lambda j: (0, 0))
    return launch(
        mlp_up,
        (h, scale, center, widen, boost),
        (like((width, tokens), BF16), like((hidden, tokens), BF16), like((tokens, hidden), BF16)),
        after,
        grid=(hidden // tile,),
        in_specs=[
            whole((tokens, width)),
            whole((1, width)),
            whole((1, width)),
            pl.BlockSpec((width, tile), lambda j: (0, j)),
            pl.BlockSpec((1, tile), lambda j: (0, j)),
        ],
        out_specs=(
            whole((width, tokens)),
            pl.BlockSpec((tile, tokens), lambda j: (j, 0)),
            pl.BlockSpec((tokens, tile), lambda j: (0, j)),
        ),
        scratch_shapes=[pltpu.VMEM((tokens, width), BF16)],
        name="mlp_up",
    )


def mlp_down(active_t_ref, shrink_ref, settle_ref, base_ref, out_ref):
    tile = 2 * LANES
    for j in range(out_ref.shape[1] // tile):
        cols = slice(j * tile, (j + 1) * tile)
        total = dot_tn(active_t_ref[...], shrink_ref[:, cols]) + settle_ref[:, cols].astype(F32)
        out_ref[:, cols] = (base_ref[:, cols] + total).astype(out_ref.dtype)


def run_mlp_down(active_t, shrink, settle, base, after):
    return launch(
        mlp_down,
        (active_t, shrink, settle, base),
        like(base.shape, BF16),
        after,
        name="mlp_down",
    )


def mlp_backward(
    grad_ref, shrink_ref, widen_ref, slope_ref,
    up_ref, boost_ref, second_ref,
):
    step = pl.program_id(0)
    active = dot_nt(grad_ref[...], shrink_ref[...])
    up = (active * slope_ref[...].astype(F32)).astype(BF16)
    up_ref[...] = up
    boost_ref[...] = jnp.sum(up.astype(F32), 0, keepdims=True)
    back = dot_nt(up, widen_ref[...])

    @pl.when(step == 0)
    def _():
        second_ref[...] = back

    @pl.when(step > 0)
    def _():
        second_ref[...] += back


def run_mlp_backward(grad, shrink, widen, slope, after, tile=512):
    tokens, width = grad.shape
    hidden = widen.shape[1]
    whole = lambda shape: pl.BlockSpec(shape, lambda j: (0, 0))
    return launch(
        mlp_backward,
        (grad, shrink, widen, slope),
        (like((tokens, hidden), BF16), like((1, hidden), F32), like((tokens, width), F32)),
        after,
        grid=(hidden // tile,),
        in_specs=[
            whole((tokens, width)),
            pl.BlockSpec((tile, width), lambda j: (j, 0)),
            pl.BlockSpec((width, tile), lambda j: (0, j)),
            pl.BlockSpec((tokens, tile), lambda j: (0, j)),
        ],
        out_specs=(
            pl.BlockSpec((tokens, tile), lambda j: (0, j)),
            pl.BlockSpec((1, tile), lambda j: (0, j)),
            whole((tokens, width)),
        ),
        flops=4 * tokens * width * hidden,
        moved=40_000_000,
        name="mlp_backward",
    )


def attention_backward(
    grad_ref, blend_ref, q_ref, k_ref, v_ref, cos_ref, low_ref, high_ref, mask_ref,
    mixed_ref, lift_ref,
    datt_ref,
):
    rows, length, _ = mask_ref.shape
    width = grad_ref.shape[1]
    head_size = width // HEADS
    tile = 2 * LANES
    for j in range(width // tile):
        cols = slice(j * tile, (j + 1) * tile)
        datt_ref[:, cols] = dot_nt(grad_ref[...], blend_ref[cols, :]).astype(BF16)

    scaled = lane_masks(head_size, head_size ** (-0.5))
    plain = lane_masks(head_size, 1.0)
    half = ROT // 2

    @pl.loop(0, rows)
    def _(r):
        at = pl.ds(pl.multiple_of(r * length, length), length)
        masked = mask_ref[r] < 0.0
        cos, low, high = cos_ref[at, :], low_ref[at, :], high_ref[at, :]

        def unturn(block):
            return (
                block * cos
                + pltpu.roll(block * low, half, 1)
                + pltpu.roll(block * high, LANES - half, 1)
            )

        lane = lax.broadcasted_iota(jnp.int32, (length, LANES), 1)
        for p in range(width // LANES):
            cols = slice(p * LANES, (p + 1) * LANES)
            query, keys, values, datt = q_ref[at, cols], k_ref[at, cols], v_ref[at, cols], datt_ref[at, cols]
            keys = stacked(keys, scaled)
            scores = dot_nt(query, keys)
            probs = softmax_halves(scores, masked)
            dprobs = dot_nt(datt, stacked(values, plain))
            draw = []
            for i, prob in enumerate(probs):
                dprob = dprobs[:, i * LANES : (i + 1) * LANES]
                draw.append((prob * (dprob - jnp.sum(prob * dprob, -1, keepdims=True))).astype(BF16))
            draw = jnp.concatenate(draw, 1)
            low_probs = jnp.concatenate([x.astype(BF16) for x in probs], 1)
            dvalues = dot_tn(low_probs, datt)
            dkeys = dot_tn(draw, query)
            dquery = dot(draw, keys)
            dvalues = jnp.where(lane < head_size, dvalues[:length], dvalues[length:])
            dkeys = jnp.where(lane < head_size, dkeys[:length], dkeys[length:]) * (head_size ** (-0.5))
            mixed_ref[at, p * LANES : (p + 1) * LANES] = unturn(dquery).astype(BF16)
            mixed_ref[at, width + p * LANES : width + (p + 1) * LANES] = unturn(dkeys).astype(BF16)
            mixed_ref[at, 2 * width + p * LANES : 2 * width + (p + 1) * LANES] = dvalues.astype(BF16)

    for j in range(3 * width // tile):
        cols = slice(j * tile, (j + 1) * tile)
        lift_ref[:, cols] = jnp.sum(mixed_ref[:, cols].astype(F32), 0, keepdims=True)

def run_attention_backward(grad, blend, q, k, v, turns, after):
    tokens, width = grad.shape
    return launch(
        attention_backward,
        (grad, blend, q, k, v, *turns),
        (like((tokens, 3 * width), BF16), like((1, 3 * width), F32)),
        after,
        flops=2 * tokens * width * width,
        moved=50_000_000,
        scratch_shapes=[pltpu.VMEM((tokens, width), BF16)],
        name="attention_backward",
    )


def stream_backward(
    grad_ref, out_grad_ref, h_ref, gain_ref, scale_ref, second_ref, packed_ref, mixed_ref,
    in_grad_ref, low_ref, vectors_ref,
    dfirst_ref,
):
    tokens, width = h_ref.shape
    length = LANES
    rows = tokens // length
    tile = 2 * LANES
    for j in range(width // tile):
        cols = slice(j * tile, (j + 1) * tile)
        dfirst_ref[:, cols] = dot_nt(mixed_ref[...], packed_ref[cols, :])

    vectors_ref[...] = jnp.zeros_like(vectors_ref)

    @pl.loop(0, rows)
    def _(r):
        at = pl.ds(pl.multiple_of(r * length, length), length)
        normed, spread = whiten(h_ref[at, :].astype(F32))
        first, second = dfirst_ref[at, :], second_ref[at, :]
        low_grad = grad_ref[at, :].astype(F32)
        for i, item in enumerate((first * normed, first, second * normed, second, low_grad)):
            vectors_ref[i : i + 1, :] += jnp.sum(item, 0, keepdims=True)
        inner = first * gain_ref[...].astype(F32) + second * scale_ref[...].astype(F32)
        inner = inner - jnp.mean(inner, -1, keepdims=True) - normed * jnp.mean(inner * normed, -1, keepdims=True)
        total = out_grad_ref[at, :].astype(F32) + inner * spread
        in_grad_ref[at, :] = total
        low_ref[at, :] = total.astype(BF16)


def run_stream_backward(grad, out_grad, h, gain, scale, second, packed, mixed, after):
    tokens, width = grad.shape
    return launch(
        stream_backward,
        (grad, out_grad, h, gain, scale, second, packed, mixed),
        (like((tokens, width), F32), like((tokens, width), BF16), like((8, width), F32)),
        after,
        flops=6 * tokens * width * width,
        moved=30_000_000,
        scratch_shapes=[pltpu.VMEM((tokens, width), F32)],
        name="stream_backward",
    )


VECTORS = (0, 1, 3, 5, 6, 7, 9, 11)


def sizes(unit):
    return (unit, unit, 3 * unit, unit, unit, unit, 4 * unit, unit)


def pack_shares(layers):
    items = [layer[i] for layer in layers for i in VECTORS]
    unit = items[0].shape[0]

    def body(*refs):
        ins, (out_ref, held) = refs[:-2], refs[-2:]
        held[...] = jnp.zeros_like(held)
        for i, item in enumerate(ins):
            held[i : i + 1, : item.shape[1]] = item[...].astype(F32)
        out_ref[...] = held[...].astype(BF16)

    return launch(
        body,
        [row(i) for i in items],
        like((unit, LANES), BF16),
        scratch_shapes=[pltpu.VMEM((unit, LANES), F32)],
        name="pack_shares",
    )


def owner_masks(devices, size):
    total = devices * size
    r = lax.broadcasted_iota(jnp.int32, (devices, total), 1)
    d = lax.broadcasted_iota(jnp.int32, (devices, total), 0) * size
    own = ((r >= d) & (r < d + size)).astype(F32)
    r = lax.broadcasted_iota(jnp.int32, (1, total), 1).astype(F32)
    r = r - jnp.floor((r + 0.5) * (1.0 / size)) * size
    lane = lax.broadcasted_iota(jnp.int32, (LANES, total), 0).astype(F32)
    return own, (lane == r).astype(BF16)


def unpack_vectors(v_ref, *refs):
    outs, held = refs[:-1], refs[-1]
    devices, unit, _ = v_ref.shape
    held[...] = v_ref[...].astype(F32)
    for size in (unit, 3 * unit, 4 * unit):
        own, lane = owner_masks(devices, size)
        for i, out_ref in enumerate(outs):
            if sizes(unit)[i % 8] == size:
                item = dot(held[:, i, :].astype(BF16), lane)
                out_ref[...] = jnp.sum(own * item, 0, keepdims=True)


def run_unpack(block):
    devices, unit, _ = block.shape
    out = launch(
        unpack_vectors,
        (block,),
        [like((1, devices * size), F32) for size in sizes(unit)] * 2,
        scratch_shapes=[pltpu.VMEM(block.shape, F32)],
        name="unpack_vectors",
    )
    return out[:8], out[8:]


def pack_gradients(vectors_ref, lift_ref, boost_ref, out_ref, held):
    devices, unit, _ = out_ref.shape
    held[...] = jnp.zeros_like(held)
    items = ((0, vectors_ref[0:1, :]), (1, vectors_ref[1:2, :]), (4, vectors_ref[2:3, :]))
    items += ((5, vectors_ref[3:4, :]), (7, vectors_ref[4:5, :]))
    for size, parts in (
        (unit, items),
        (3 * unit, ((2, lift_ref[...]),)),
        (4 * unit, ((6, boost_ref[...]),)),
    ):
        own, lane = owner_masks(devices, size)
        for i, value in parts:
            held[:, i, :] = dot_nt((own * value).astype(BF16), lane)
    out_ref[...] = held[...].astype(BF16)


def run_pack(vectors, lift, boost, devices):
    shape = (devices, vectors.shape[1] // devices, LANES)
    return launch(
        pack_gradients,
        (vectors, lift, boost),
        like(shape, BF16),
        scratch_shapes=[pltpu.VMEM(shape, F32)],
        name="pack_gradients",
    )


WIDE, NARROW = "wide", "narrow"


def flip(item, bit):
    return lax.ppermute(item, WIDE, [(i, i ^ bit) for i in range(8)])


def across_core(item):
    return flip(item, 1)


def across_x(item):
    return flip(item, 2)


def across_y(item):
    return flip(item, 4)


def along_z(item, step):
    return lax.ppermute(item, NARROW, [(i, (i + step) % 4) for i in range(4)])


def beside_kernel(items, outs):
    def body(*refs):
        ins, targets = refs[:items], refs[items:]
        at = [0] * outs
        for i, item in enumerate(ins):
            o = min(i, outs - 1)
            height, width = targets[o].shape[0], item.shape[1]
            for q in range(item.shape[0] // height):
                targets[o][:, at[o] : at[o] + width] = item[q * height : (q + 1) * height, :]
                at[o] += width

    return body


def beside(items, unit, after=()):
    width = sum(i.shape[0] // unit * i.shape[1] for i in items)
    return launch(
        beside_kernel(len(items), 1), items, like((unit, width), BF16), after, moved=400_000, name="beside"
    )


def stack_kernel(slot_ref, *refs):
    out_ref = refs[-1]
    for i, item in enumerate(refs[:-1]):
        out_ref[slot_ref[i]] = item[...]


SMEM = pl.BlockSpec(memory_space=pltpu.SMEM)
VMEM = pl.BlockSpec(memory_space=pltpu.VMEM)


class Gather:

    def __init__(self, share):
        self.share = share
        self.ring = [share] + [along_z(share, k) for k in (1, 2, 3)]

    def plane(self, where, after=()):
        z = where[2]
        slots = jnp.stack([(z - k) % 4 for k in range(4)]).astype(jnp.int32)
        self.own = self.token = launch(
            stack_kernel,
            (slots, *self.ring),
            like((4,) + self.share.shape, BF16),
            after,
            in_specs=[SMEM] + [VMEM] * 4,
            name="stack_ring",
        )
        self.left, self.up = across_x(self.own), across_y(self.own)
        self.near = (self.left, self.up)

    def corner(self):
        self.far = (across_x(self.up[:2]), across_y(self.left[2:]))
        self.mine = (self.own, self.left, self.up) + self.far
        self.other = tuple(across_core(m) for m in self.mine)


def assemble_kernel(widths):
    def body(slot_ref, *refs):
        pieces, outs = refs[:10], refs[10:]
        for i, piece in enumerate(pieces):
            side, i = divmod(i, 5)
            slot = slot_ref[side * 4 + min(i, 3)]
            first = 2 if i == 4 else 0
            for z in range(piece.shape[0]):
                start = 0
                for out, width in zip(outs, widths):
                    if len(out.shape) == 5:
                        part = out.shape[-1]
                        for q in range(width // part):
                            cols = slice(start + q * part, start + (q + 1) * part)
                            out[slot, first + z, q] = piece[z, :, cols]
                    else:
                        out[slot, first + z] = piece[z, :, start : start + width]
                    start += width

    return body


def assemble(gathered, where, widths, folds, after=()):
    mine, other = gathered.mine, gathered.other
    plane, core, _ = where
    slots = jnp.stack(
        [(plane ^ r) * 2 + c for c in (core, 1 - core) for r in range(4)]
    ).astype(jnp.int32)
    unit = mine[0].shape[1]
    shapes = [
        like((8, 4, f, unit, w // f) if f > 1 else (8, 4, unit, w), BF16)
        for w, f in zip(widths, folds)
    ]
    outs = launch(
        assemble_kernel(widths),
        (slots, *mine, *other),
        shapes,
        after,
        in_specs=[SMEM] + [VMEM] * 10,
        moved=10_000_000,
        name="assemble",
    )
    return [o.reshape(-1, o.shape[-1]) for o in outs]


def half_kernel(first_tiles, tiles, own, extra):
    def body(index_ref, *refs):
        step = pl.program_id(0)
        pairs = 1 if first_tiles == tiles else 2
        refs = list(refs)
        terms = [(refs.pop(0), refs.pop(0)) for _ in range(pairs)]
        extra_ref = refs.pop(0) if extra else None
        arrived = refs.pop(0) if own else None
        keeps = refs[-pairs:]
        outs = refs[:-pairs]

        @pl.when(step == 0)
        def _():
            for (left, _), keep in zip(terms, keeps):
                size = left.shape[0] // 8
                for r in range(4):
                    at = pl.ds(pl.multiple_of(index_ref[r] * size, size), size)
                    keep[r * size : (r + 1) * size, :] = left[at, :]

        def emit(total):
            if not own:
                outs[0][...] = total.astype(BF16)
                return
            total = (total.astype(F32) + arrived[...].astype(F32)).astype(BF16)
            p_ref, x_ref, y_ref, xp_ref, yp_ref = outs
            p_ref[...] = total[0]
            x_ref[0] = total[3, :2]
            x_ref[1] = total[1, :2]
            xp_ref[...] = total[1, 2:]
            y_ref[0] = total[3, 2:]
            y_ref[1] = total[2, 2:]
            yp_ref[...] = total[2, :2]

        def product(i):
            keep = keeps[i]
            total = dot(keep[...], terms[i][1][...])
            emit(total.reshape(4, 4, keep.shape[0] // 16, total.shape[1]))

        if pairs == 1:
            product(0)
            return
        pl.when(step < first_tiles)(lambda: product(0))
        pl.when((step >= first_tiles) & (step < tiles))(lambda: product(1))
        if extra:

            @pl.when(step == tiles)
            def _():
                total = jnp.stack([extra_ref[index_ref[r]] for r in range(4)])
                width = outs[0].shape[-1] - total.shape[-1]
                emit(jnp.concatenate([total, jnp.zeros(total.shape[:-1] + (width,), BF16)], -1))

    return body


def run_half(index, lefts, rights, extra, arrived, after=(), tile=384):
    own = arrived is not None
    unit = lefts[0].shape[0] // 32
    tokens = lefts[0].shape[1]
    counts = [r.shape[1] // tile for r in rights]
    first_tiles, tiles = counts[0], sum(counts)
    columns = tiles * tile + (0 if extra is None else LANES)
    block = lambda *shape: like(shape + (unit, columns), BF16)
    spec = lambda *shape: pl.BlockSpec(
        shape + (unit, tile), lambda j: (0,) * len(shape) + (0, j)
    )
    if own:
        shapes = (block(4), block(2, 2), block(2, 2), block(2), block(2))
        out_specs = (spec(4), spec(2, 2), spec(2, 2), spec(2), spec(2))
    else:
        shapes, out_specs = block(4, 4), spec(4, 4)
    operands, in_specs = [index], [SMEM]
    start = 0
    for left, right, count in zip(lefts, rights, counts):
        operands += [left, right]
        in_specs += [
            pl.BlockSpec(left.shape, lambda j: (0, 0)),
            pl.BlockSpec(
                (tokens, tile),
                lambda j, start=start, count=count: (0, jnp.clip(j - start, 0, count - 1)),
            ),
        ]
        start += count
    if extra is not None:
        operands.append(extra.reshape(8, 4, unit, LANES))
        in_specs.append(VMEM)
    if own:
        operands.append(arrived)
        in_specs.append(spec(4, 4))
    return launch(
        half_kernel(first_tiles, tiles, own, extra is not None),
        operands,
        shapes,
        after,
        grid=(tiles + (0 if extra is None else 1),),
        in_specs=in_specs,
        out_specs=out_specs,
        scratch_shapes=[pltpu.VMEM((16 * unit, tokens), BF16) for _ in lefts],
        flops=2 * tokens * 16 * unit * columns,
        moved=20_000_000,
        name="own_half" if own else "other_half",
    )


def add_kernel(a_ref, b_ref, c_ref, d_ref, x_ref, y_ref):
    x_ref[...] = (a_ref[...].astype(F32) + b_ref[...].astype(F32)).astype(BF16)
    y_ref[...] = (c_ref[...].astype(F32) + d_ref[...].astype(F32)).astype(BF16)


def join_kernel(z_ref, p_ref, x1_ref, y2_ref, y1_ref, x2_ref, *refs):
    outs, held = refs[:4], refs[4]
    held[0:2] = p_ref[0:2].astype(F32) + x1_ref[1].astype(F32) + y2_ref[...].astype(F32)
    held[2:4] = p_ref[2:4].astype(F32) + y1_ref[1].astype(F32) + x2_ref[...].astype(F32)
    for k, out in enumerate(outs):
        out[...] = held[z_ref[k]].astype(BF16)


class Scatter:

    def __init__(self, lefts, rights, extra, where, after):
        plane, core, self.z = where
        other = jnp.stack([(plane ^ r) * 2 + 1 - core for r in range(4)]).astype(jnp.int32)
        self.mine = jnp.stack([(plane ^ r) * 2 + core for r in range(4)]).astype(jnp.int32)
        self.terms = lefts, rights, extra
        self.token = run_half(other, lefts, rights, extra, None, after)
        self.arrived = across_core(self.token)

    def own(self, after):
        self.p, x, y, self.xp, self.yp = run_half(self.mine, *self.terms, self.arrived, after)
        self.token = self.p
        self.x1, self.y1 = across_x(x), across_y(y)

    def far(self, after):
        shape = like(self.xp.shape, BF16)
        xs, ys = launch(
            lambda a, b, c, d, o, q: add_kernel(a, b.at[0], c, d.at[0], o, q),
            (self.xp, self.y1, self.yp, self.x1),
            (shape, shape),
            after,
            name="add_far",
        )
        self.token = xs
        self.x2, self.y2 = across_x(xs), across_y(ys)

    def join(self, after):
        turn = jnp.stack([(self.z + k) % 4 for k in range(4)]).astype(jnp.int32)
        shape = like(self.p.shape[1:], BF16)
        blocks = launch(
            join_kernel,
            (turn, self.p, self.x1, self.y2, self.y1, self.x2),
            (shape,) * 4,
            after,
            in_specs=[SMEM] + [VMEM] * 5,
            scratch_shapes=[pltpu.VMEM(self.p.shape, F32)],
            name="join_plane",
        )
        self.token = blocks[0]
        self.got = [blocks[0]] + [along_z(blocks[k], k) for k in (1, 2, 3)]

    def finish(self, widths, after):
        unit, columns = self.got[0].shape
        outs = launch(
            sum_kernel(widths),
            self.got,
            [like((unit, w), F32) for w in widths],
            after,
            name="sum_ring",
        )
        self.token = outs[0]
        self.sums = outs


def sum_kernel(widths):
    def body(a, b, c, d, *outs):
        start = 0
        for out, width in zip(outs, widths):
            cols = slice(start, start + width)
            out[...] = (
                a[:, cols].astype(F32)
                + b[:, cols].astype(F32)
                + c[:, cols].astype(F32)
                + d[:, cols].astype(F32)
            )
            start += width

    return body


def row(item):
    return item.reshape(1, -1)


def on_cube(stream, cotangent, segment_ids, *weights):
    one, two = weights[:12], weights[12:]
    unit = one[0].shape[0]
    count, length, width = stream.shape
    tokens = count * length
    hidden = 4 * width
    fold = hidden // width
    wide = lax.axis_index(WIDE)
    where = (wide // 2, wide % 2, lax.axis_index(NARROW))
    head_parts, tail_parts = (3 * width, width), (hidden, hidden)

    h1 = Gather(beside([one[2], one[4], pack_shares((one, two))], unit))
    h1.plane(where)
    t1 = Gather(beside([one[8], one[10]], unit, (h1.token,)))
    h1.corner()
    turns = tables(segment_ids, width // HEADS)
    t1.plane(where, h1.far)
    h2 = Gather(beside([two[2], two[4]], unit, (t1.token,)))
    packed, blend, block = assemble(
        h1, where, head_parts + (LANES,), (1, 1, 1), (h2.share,)
    )
    vecs = run_unpack(block.reshape(32, unit, LANES))
    h = stream.reshape(tokens, width)
    gain, shift, lift, nudge, scale, center, boost, settle = vecs[0]
    first_t, q, k, v, att_t, base = run_attention_forward(
        h, gain, shift, packed, lift, turns, blend, nudge, ()
    )
    w2 = Gather(beside([two[8]], unit, (base, *h2.ring[1:])))
    t1.corner()
    h2.plane(where, (w2.share, *t1.far))
    s2 = Gather(beside([two[10]], unit, (h2.token, *w2.ring[1:])))
    widen, shrink = assemble(t1, where, tail_parts, (1, fold), (s2.share,))
    second_t, active_t, slope, middle = run_mlp_forward(
        h, scale, center, widen, boost, shrink, settle, base, ()
    )
    saved = [(h, first_t, q, k, v, att_t, second_t, active_t, slope)]
    mats = [(packed, blend, widen, shrink)]

    h2.corner()
    w2.plane(where, (middle, *h2.far))
    packed, blend = assemble(h2, where, head_parts, (1, 1), (w2.token,))
    gain, shift, lift, nudge, scale, center, boost, settle = vecs[1]
    first_t, q, k, v, att_t, base = run_attention_forward(
        middle, gain, shift, packed, lift, turns, blend, nudge, ()
    )
    w2.corner()
    s2.plane(where, (base, *w2.far))
    (widen,) = assemble(w2, where, (hidden,), (1,), (s2.token,))
    second_t, active_t, slope = run_mlp_up(middle, scale, center, widen, boost, ())
    grad = low = cotangent.reshape(tokens, width)
    s2.corner()
    gs2 = Scatter([active_t], [low], None, where, s2.near)
    gs2.own((gs2.token,))
    (shrink,) = assemble(s2, where, (hidden,), (fold,), (gs2.token,))

    wide_parts = (3 * width, width, LANES)
    up, g_boost, back = run_mlp_backward(low, shrink, widen, slope, (gs2.token,))
    gs2.far((back,))
    gw2 = Scatter([second_t], [up], None, where, (gs2.token,))
    gw2.own((gw2.token, gs2.x2, gs2.y2))
    gs2.join((gw2.token,))
    mixed, g_lift = run_attention_backward(low, blend, q, k, v, turns, (gs2.token,))
    gw2.far((mixed, *gs2.got[1:]))
    gs2.finish((width,), (gw2.token,))
    grad, low_one, vectors = run_stream_backward(
        low, grad, middle, gain, scale, back, packed, mixed, (gs2.token,)
    )
    gw2.join((grad,))
    extra = run_pack(vectors, g_lift, g_boost, 32)
    gp2 = Scatter([first_t, att_t], [mixed, low], extra, where, (gw2.token,))
    last = active_t, shrink, settle, base

    low = low_one
    h, first_t, q, k, v, att_t, second_t, active_t, slope = saved[0]
    packed, blend, widen, shrink = mats[0]
    gs1 = Scatter([active_t], [low], None, where, (gp2.token,))
    gp2.own((gs1.token,))
    gs1.own((gp2.token,))
    up, g_boost, back = run_mlp_backward(low, shrink, widen, slope, (gs1.token,))
    gp2.far((back, *gw2.got[1:]))
    gw2.finish((hidden,), (gp2.token,))
    gw1 = Scatter([second_t], [up], None, where, (gw2.token,))
    gs1.far((gw1.token,))
    gw1.own((gs1.token, gp2.x2, gp2.y2))
    gp2.join((gw1.token,))
    mixed, g_lift = run_attention_backward(low, blend, q, k, v, turns, (gp2.token,))
    gs1.join((mixed,))
    gw1.far((gs1.token, *gp2.got[1:]))
    gp2.finish(wide_parts, (gw1.token,))
    gain, scale = vecs[0][0], vecs[0][4]
    grad, _, vectors = run_stream_backward(
        low, grad, h, gain, scale, back, packed, mixed, (gp2.token,)
    )
    extra = run_pack(vectors, g_lift, g_boost, 32)
    gp1 = Scatter([first_t, att_t], [mixed, low], extra, where, (*gs1.got[1:],))
    gw1.join((gp1.token,))
    gp1.own((gw1.token,))
    gs1.finish((width,), (gp1.token,))
    ending = run_mlp_down(*last, (gs1.token,))
    gp1.far((ending,))
    gw1.finish((hidden,), (gp1.token,))
    gp1.join((gw1.token,))
    gp1.finish(wide_parts, (gp1.token,))

    out = []
    for p, w, s in ((gp1, gw1, gs1), (gp2, gw2, gs2)):
        g = [None] * 12
        g[2], g[4], block = p.sums
        (g[8],), (g[10],) = w.sums, s.sums
        for r, (i, size) in enumerate(zip(VECTORS, sizes(unit))):
            g[i] = block[r, :size]
        g[5] = g[11]
        out += g
    shape = (count, length, width)
    return (ending.reshape(shape), grad.reshape(shape)) + tuple(out)


def whole(item):
    return lax.all_gather(item, (WIDE, NARROW), axis=0, tiled=True)


def owned(item):
    for axis in (WIDE, NARROW):
        parts = lax.axis_size(axis)
        item = item.reshape((parts, item.shape[0] // parts) + item.shape[1:])
        item = lax.all_to_all(item.astype(BF16), axis, 0, 0, tiled=True)
        item = jnp.sum(item.astype(F32), 0)
    return item


def on_any(stream, cotangent, segment_ids, *weights):
    count, length, width = stream.shape
    tokens = count * length
    turns = tables(segment_ids, width // HEADS)
    h = stream.reshape(tokens, width)
    kept = []
    for layer in (weights[:12], weights[12:]):
        w = [whole(i) for i in layer]
        gain, shift, lift, nudge, scale, center, boost, settle = (row(w[i]) for i in VECTORS)
        packed, blend, widen, shrink = w[2], w[4], w[8], w[10]
        first_t, q, k, v, att_t, base = run_attention_forward(
            h, gain, shift, packed, lift, turns, blend, nudge, ()
        )
        second_t, active_t, slope, out = run_mlp_forward(
            h, scale, center, widen, boost, shrink, settle, base, ()
        )
        mats = gain, scale, packed, blend, widen, shrink
        kept.append((mats, h, first_t, q, k, v, att_t, second_t, active_t, slope))
        h = out
    result = h.astype(BF16).reshape(stream.shape)
    grad = low = cotangent.reshape(tokens, width)
    out = ()
    for mats, h, first_t, q, k, v, att_t, second_t, active_t, slope in reversed(kept):
        gain, scale, packed, blend, widen, shrink = mats
        up, g_boost, back = run_mlp_backward(low, shrink, widen, slope, ())
        mixed, g_lift = run_attention_backward(low, blend, q, k, v, turns, ())
        grad, next_low, vectors = run_stream_backward(
            low, grad, h, gain, scale, back, packed, mixed, ()
        )
        g_gain, g_shift, g_scale, g_center, g_settle = (owned(vectors[i]) for i in range(5))
        out = (
            g_gain,
            g_shift,
            owned(dot(first_t, mixed)),
            owned(g_lift[0]),
            owned(dot(att_t, low)),
            g_settle,
            g_scale,
            g_center,
            owned(dot(second_t, up)),
            owned(g_boost[0]),
            owned(dot(active_t, low)),
            g_settle,
        ) + out
        low = next_low
    return (result, grad.reshape(stream.shape)) + out


def solution(mesh):
    axes = (WIDE, NARROW)
    one, two, three = P(axes), P(axes, None), P(axes, None, None)
    layer = (one, one, two, one, two, one, one, one, two, one, two, one)
    cube = dict(mesh.shape) == {WIDE: 8, NARROW: 4}
    return jax.shard_map(
        on_cube if cube else on_any,
        mesh=mesh,
        in_specs=(three, three, two) + layer + layer,
        out_specs=(three, three) + layer + layer,
        check_vma=False,
    )
```

```python
import jax
import jax.numpy as jnp
from jax import lax
from jax.experimental import pallas as pl
from jax.experimental.pallas import tpu as pltpu
from jax.sharding import PartitionSpec as P

HEADS = 12
ROT = 16
EPS = 1e-05
F32 = jnp.float32
BF16 = jnp.bfloat16
LANES = 128
COVER = 20
SMALL = 30
MASKED = -1000000000.0
VMEM_LIMIT = 24 * 1024 * 1024
WIDE, NARROW = "wide", "narrow"
SMEM = pl.BlockSpec(memory_space=pltpu.SMEM)
VMEM = pl.BlockSpec(memory_space=pltpu.VMEM)
ANY = pl.BlockSpec(memory_space=pl.ANY)
VECTORS = (0, 1, 3, 5, 6, 7, 9, 11)
GAIN, SHIFT, LIFT, NUDGE, SCALE, CENTER, BOOST, SETTLE = range(8)


def like(shape, kind):
    return jax.ShapeDtypeStruct(tuple(shape), kind)


def fence(*items):
    return lax.optimization_barrier(items)


ISSUED = {}


def launch(
    body, operands, out_shape, after=(), in_specs=None, out_specs=None, cover=SMALL,
    limit=VMEM_LIMIT, **more
):
    operands = list(operands)
    several = isinstance(out_shape, (list, tuple))
    outs = list(out_shape) if several else [out_shape]
    if in_specs is None:
        in_specs = [VMEM] * len(operands)
    if out_specs is None:
        out_specs = [VMEM] * len(outs)
    elif not isinstance(out_specs, (list, tuple)):
        out_specs = [out_specs]
    waits, specs = [], []
    for item in jax.tree.leaves(after):
        small = ISSUED.get(id(item))
        small = (item, ANY) if small is None else (small[1], VMEM)
        if all(small[0] is not w for w in waits):
            waits.append(small[0])
            specs.append(small[1])
    count = len(operands)
    first = count + len(waits)
    grid = "grid" in more

    def kernel(*refs):
        end = first + len(outs)
        refs[end][...] = jnp.zeros_like(refs[end])
        body(*refs[:count], *refs[first:end], *refs[end + 1 :])

    signal = like((8, LANES), F32)
    whole = pl.BlockSpec((8, LANES), lambda j: (0, 0)) if grid else VMEM
    if grid:
        specs = [whole if s is VMEM else s for s in specs]
    results = pl.pallas_call(
        kernel,
        out_shape=(*outs, signal),
        in_specs=[*in_specs, *specs],
        out_specs=(*out_specs, whole),
        compiler_params=pltpu.CompilerParams(vmem_limit_bytes=limit),
        cost_estimate=pl.CostEstimate(
            flops=int(cover * 1e9), bytes_accessed=1000, transcendentals=0
        ),
        **more,
    )(*operands, *waits)
    for item in results[:-1]:
        ISSUED[id(item)] = item, results[-1]
    return results[:-1] if several else results[0]


def dot(left, right):
    return lax.dot_general(left, right, (((1,), (0,)), ((), ())), preferred_element_type=F32)


def dot_nt(left, right):
    return lax.dot_general(left, right, (((1,), (1,)), ((), ())), preferred_element_type=F32)


def dot_tn(left, right):
    return lax.dot_general(left, right, (((0,), (0,)), ((), ())), preferred_element_type=F32)


def tables(segments, head_size):
    length = segments.shape[-1]
    before = jnp.sum((segments[:, None, :] < segments[:, :, None]).astype(jnp.int32), -1)
    place = jnp.arange(length, dtype=jnp.int32)
    position = (place[None, :] - before).astype(F32).reshape(-1, 1)
    half = ROT // 2
    lane = jnp.arange(LANES, dtype=jnp.int32) % head_size
    freqs = 10000.0 ** (-((lane % half).astype(F32) * 2.0 / ROT))
    angle = position * freqs[None, :]
    lane = lane[None, :]
    cosine = jnp.where(lane < ROT, jnp.cos(angle), 1.0)
    sine = jnp.sin(angle)
    low = jnp.where(lane < half, -sine, 0.0)
    high = jnp.where((lane >= half) & (lane < ROT), sine, 0.0)
    allowed = (segments[:, :, None] == segments[:, None, :]) & (place[:, None] >= place[None, :])[
        None
    ]
    return jnp.stack([cosine, low, high]), jnp.where(allowed, 0.0, -1.0).astype(F32)


def whiten(x):
    centered = x - jnp.mean(x, -1, keepdims=True)
    spread = jnp.mean(centered * centered, -1, keepdims=True)
    scale = lax.rsqrt(spread + EPS)
    return centered * scale, scale


def vector(vec_ref, layer, which, cols):
    at = layer * 8 + which
    return vec_ref[at : at + 1, cols]


def lane_masks(head_size, value):
    lane = lax.broadcasted_iota(jnp.int32, (1, LANES), 1)
    return [
        jnp.where((lane >= i * head_size) & (lane < (i + 1) * head_size), value, 0.0).astype(BF16)
        for i in range(LANES // head_size)
    ]


def stacked(block, masks):
    return jnp.concatenate([block * m for m in masks], 0)


def softmax_halves(scores, masked):
    out = []
    for i in range(scores.shape[1] // LANES):
        logits = jnp.where(masked, MASKED, scores[:, i * LANES : (i + 1) * LANES])
        expo = jnp.exp(logits - jnp.max(logits, -1, keepdims=True))
        out.append(expo * (1.0 / jnp.sum(expo, -1, keepdims=True)))
    return out


def norm_rows(h_ref, vec_ref, layer, which, out_ref, out_t_ref):
    tokens, width = h_ref.shape
    cols = slice(0, width)

    @pl.loop(0, tokens // LANES)
    def _(r):
        at = pl.ds(pl.multiple_of(r * LANES, LANES), LANES)
        normed, _ = whiten(h_ref[at, :].astype(F32))
        item = normed * vector(vec_ref, layer, which, cols)
        item = (item + vector(vec_ref, layer, which + 1, cols)).astype(BF16)
        out_ref[at, :] = item
        out_t_ref[:, at] = item.T


def run_attention_forward(layer, h, vec, packed, blend, turns, mask, after=()):
    tokens, width = h.shape
    head_size = width // HEADS
    rows, length, _ = mask.shape

    def body(
        h_ref, vec_ref, packed_ref, blend_ref, turn_ref, mask_ref,
        first_t_ref, q_ref, k_ref, v_ref, att_t_ref, base_ref,
        first_ref, att_ref,
    ):
        norm_rows(h_ref, vec_ref, layer, GAIN, first_ref, first_t_ref)
        tile = 2 * LANES
        for j in range(width // tile):
            for part, out_ref in enumerate((q_ref, k_ref, v_ref)):
                cols = slice(part * width + j * tile, part * width + (j + 1) * tile)
                mixed = dot(first_ref[...], packed_ref[:, cols])
                mixed = mixed + vector(vec_ref, layer, LIFT, cols)
                for b in range(tile // LANES):
                    block = mixed[:, b * LANES : (b + 1) * LANES]
                    if part < 2:
                        block = (
                            block * turn_ref[0]
                            + pltpu.roll(block, LANES - ROT // 2, 1) * turn_ref[1]
                            + pltpu.roll(block, ROT // 2, 1) * turn_ref[2]
                        )
                    start = j * tile + b * LANES
                    out_ref[:, start : start + LANES] = block.astype(BF16)

        scaled = lane_masks(head_size, head_size ** (-0.5))
        plain = lane_masks(head_size, 1.0)

        @pl.loop(0, rows)
        def _(r):
            at = pl.ds(pl.multiple_of(r * length, length), length)
            masked = mask_ref[r] < 0.0
            for p in range(width // LANES):
                cols = slice(p * LANES, (p + 1) * LANES)
                scores = dot_nt(q_ref[at, cols], stacked(k_ref[at, cols], scaled))
                probs = [p.astype(BF16) for p in softmax_halves(scores, masked)]
                probs = jnp.concatenate(probs, 1)
                attended = dot(probs, stacked(v_ref[at, cols], plain)).astype(BF16)
                att_ref[at, cols] = attended
                att_t_ref[cols, at] = attended.T

        for j in range(width // tile):
            cols = slice(j * tile, (j + 1) * tile)
            base_ref[:, cols] = (
                h_ref[:, cols].astype(F32)
                + dot(att_ref[...], blend_ref[:, cols])
                + vector(vec_ref, layer, NUDGE, cols)
            )

    square = like((tokens, width), BF16)
    turned = like((width, tokens), BF16)
    return launch(
        body,
        (h, vec, packed, blend, turns, mask),
        (turned, square, square, square, turned, like((tokens, width), F32)),
        after,
        scratch_shapes=[pltpu.VMEM((tokens, width), BF16)] * 2,
        cover=COVER,
        name="attention_forward",
    )


def gelu_pair(u):
    z = jnp.abs(u) * 0.7071067811865476
    t = 1.0 / (1.0 + 0.3275911 * z)
    poly = t * (
        0.127414796
        + t * (-0.142248368 + t * (0.7107068705 + t * (-0.7265760135 + t * 0.5307027145)))
    )
    bell = jnp.exp(-0.5 * u * u)
    tail = poly * bell
    cdf = jnp.where(u < 0.0, tail, 1.0 - tail)
    return u * cdf, cdf + u * bell * 0.3989422804014327


def run_mlp_up(layer, h, vec, widen, after=(), tile=512):
    tokens, width = h.shape
    hidden = widen.shape[1]

    def body(h_ref, vec_ref, widen_ref, second_t_ref, active_t_ref, slope_ref, second_ref):
        step = pl.program_id(0)

        @pl.when(step == 0)
        def _():
            norm_rows(h_ref, vec_ref, layer, SCALE, second_ref, second_t_ref)

        cols = pl.ds(pl.multiple_of(step * tile, tile), tile)
        upward = dot(second_ref[...], widen_ref[...]) + vector(vec_ref, layer, BOOST, cols)
        active, slope = gelu_pair(upward)
        slope_ref[...] = slope.astype(BF16)
        active_t_ref[...] = active.astype(BF16).T

    whole = lambda shape: pl.BlockSpec(shape, lambda j: (0, 0))
    return launch(
        body,
        (h, vec, widen),
        (like((width, tokens), BF16), like((hidden, tokens), BF16), like((tokens, hidden), BF16)),
        after,
        grid=(hidden // tile,),
        in_specs=[
            whole((tokens, width)),
            whole(vec.shape),
            pl.BlockSpec((width, tile), lambda j: (0, j)),
        ],
        out_specs=(
            whole((width, tokens)),
            pl.BlockSpec((tile, tokens), lambda j: (j, 0)),
            pl.BlockSpec((tokens, tile), lambda j: (0, j)),
        ),
        scratch_shapes=[pltpu.VMEM((tokens, width), BF16)],
        cover=COVER,
        name="mlp_up",
    )


def run_mlp_down(layer, active_t, shrink, vec, base, kind, after=()):
    def body(active_t_ref, shrink_ref, vec_ref, base_ref, out_ref):
        tile = 2 * LANES
        for j in range(out_ref.shape[1] // tile):
            cols = slice(j * tile, (j + 1) * tile)
            total = dot_tn(active_t_ref[...], shrink_ref[:, cols])
            total = total + vector(vec_ref, layer, SETTLE, cols)
            out_ref[:, cols] = (base_ref[:, cols] + total).astype(out_ref.dtype)

    return launch(
        body, (active_t, shrink, vec, base), like(base.shape, kind), after, cover=COVER, name="mlp_down"
    )


def run_mlp_backward(grad, shrink, widen, slope, after=(), tile=512):
    tokens, width = grad.shape
    hidden = widen.shape[1]

    def body(grad_ref, shrink_ref, widen_ref, slope_ref, up_ref, boost_ref, second_ref):
        step = pl.program_id(0)
        active = dot_nt(grad_ref[...], shrink_ref[...])
        up = (active * slope_ref[...].astype(F32)).astype(BF16)
        up_ref[...] = up
        boost_ref[...] = jnp.sum(up.astype(F32), 0, keepdims=True)
        back = dot_nt(up, widen_ref[...])

        @pl.when(step == 0)
        def _():
            second_ref[...] = back

        @pl.when(step > 0)
        def _():
            second_ref[...] += back

    whole = lambda shape: pl.BlockSpec(shape, lambda j: (0, 0))
    return launch(
        body,
        (grad, shrink, widen, slope),
        (like((tokens, hidden), BF16), like((1, hidden), F32), like((tokens, width), F32)),
        after,
        grid=(hidden // tile,),
        in_specs=[
            whole((tokens, width)),
            pl.BlockSpec((tile, width), lambda j: (j, 0)),
            pl.BlockSpec((width, tile), lambda j: (0, j)),
            pl.BlockSpec((tokens, tile), lambda j: (0, j)),
        ],
        out_specs=(
            pl.BlockSpec((tokens, tile), lambda j: (0, j)),
            pl.BlockSpec((1, tile), lambda j: (0, j)),
            whole((tokens, width)),
        ),
        cover=COVER,
        name="mlp_backward",
    )


def run_attention_backward(grad, blend, q, k, v, turns, mask, after=()):
    tokens, width = grad.shape
    head_size = width // HEADS
    rows, length, _ = mask.shape

    def body(
        grad_ref, blend_ref, q_ref, k_ref, v_ref, turn_ref, mask_ref, mixed_ref, lift_ref, datt_ref
    ):
        tile = 2 * LANES
        for j in range(width // tile):
            cols = slice(j * tile, (j + 1) * tile)
            datt_ref[:, cols] = dot_nt(grad_ref[...], blend_ref[cols, :]).astype(BF16)

        scaled = lane_masks(head_size, head_size ** (-0.5))
        plain = lane_masks(head_size, 1.0)

        @pl.loop(0, rows)
        def _(r):
            at = pl.ds(pl.multiple_of(r * length, length), length)
            masked = mask_ref[r] < 0.0
            cos, low, high = turn_ref[0, at, :], turn_ref[1, at, :], turn_ref[2, at, :]

            def unturn(block):
                return (
                    block * cos
                    + pltpu.roll(block * low, ROT // 2, 1)
                    + pltpu.roll(block * high, LANES - ROT // 2, 1)
                )

            lane = lax.broadcasted_iota(jnp.int32, (length, LANES), 1)
            for p in range(width // LANES):
                cols = slice(p * LANES, (p + 1) * LANES)
                query, values, datt = q_ref[at, cols], v_ref[at, cols], datt_ref[at, cols]
                keys = stacked(k_ref[at, cols], scaled)
                probs = softmax_halves(dot_nt(query, keys), masked)
                dprobs = dot_nt(datt, stacked(values, plain))
                draw = []
                for i, prob in enumerate(probs):
                    dprob = dprobs[:, i * LANES : (i + 1) * LANES]
                    inner = jnp.sum(prob * dprob, -1, keepdims=True)
                    draw.append((prob * (dprob - inner)).astype(BF16))
                draw = jnp.concatenate(draw, 1)
                low_probs = jnp.concatenate([x.astype(BF16) for x in probs], 1)
                dvalues = dot_tn(low_probs, datt)
                dkeys = dot_tn(draw, query)
                dquery = dot(draw, keys)
                dvalues = jnp.where(lane < head_size, dvalues[:length], dvalues[length:])
                dkeys = jnp.where(lane < head_size, dkeys[:length], dkeys[length:])
                dkeys = dkeys * (head_size ** (-0.5))
                for part, item in enumerate((unturn(dquery), unturn(dkeys), dvalues)):
                    start = part * width + p * LANES
                    mixed_ref[at, start : start + LANES] = item.astype(BF16)

        for j in range(3 * width // tile):
            cols = slice(j * tile, (j + 1) * tile)
            lift_ref[:, cols] = jnp.sum(mixed_ref[:, cols].astype(F32), 0, keepdims=True)

    return launch(
        body,
        (grad, blend, q, k, v, turns, mask),
        (like((tokens, 3 * width), BF16), like((1, 3 * width), F32)),
        after,
        scratch_shapes=[pltpu.VMEM((tokens, width), BF16)],
        cover=COVER,
        name="attention_backward",
    )


def run_stream_backward(layer, grad, out_grad, h, vec, second, packed, mixed, after=()):
    tokens, width = grad.shape

    def body(
        grad_ref, out_grad_ref, h_ref, vec_ref, second_ref, packed_ref, mixed_ref,
        in_grad_ref, low_ref, sums_ref,
        dfirst_ref,
    ):
        tile = 2 * LANES
        for j in range(width // tile):
            cols = slice(j * tile, (j + 1) * tile)
            dfirst_ref[:, cols] = dot_nt(mixed_ref[...], packed_ref[cols, :])
        sums_ref[...] = jnp.zeros_like(sums_ref)
        cols = slice(0, width)

        @pl.loop(0, tokens // LANES)
        def _(r):
            at = pl.ds(pl.multiple_of(r * LANES, LANES), LANES)
            normed, spread = whiten(h_ref[at, :].astype(F32))
            first, second = dfirst_ref[at, :], second_ref[at, :]
            low_grad = grad_ref[at, :].astype(F32)
            for i, item in enumerate((first * normed, first, second * normed, second, low_grad)):
                sums_ref[i : i + 1, :] += jnp.sum(item, 0, keepdims=True)
            inner = first * vector(vec_ref, layer, GAIN, cols)
            inner = inner + second * vector(vec_ref, layer, SCALE, cols)
            along = jnp.mean(inner * normed, -1, keepdims=True)
            inner = inner - jnp.mean(inner, -1, keepdims=True) - normed * along
            total = out_grad_ref[at, :].astype(F32) + inner * spread
            in_grad_ref[at, :] = total
            low_ref[at, :] = total.astype(BF16)

    return launch(
        body,
        (grad, out_grad, h, vec, second, packed, mixed),
        (like((tokens, width), F32), like((tokens, width), BF16), like((8, width), F32)),
        after,
        scratch_shapes=[pltpu.VMEM((tokens, width), F32)],
        cover=COVER,
        name="stream_backward",
    )


def sizes(unit):
    return (unit, unit, 3 * unit, unit, unit, unit, 4 * unit, unit)


def row(item):
    return item.reshape(1, -1)


def owner_masks(devices, size):
    total = devices * size
    r = lax.broadcasted_iota(jnp.int32, (devices, total), 1)
    d = lax.broadcasted_iota(jnp.int32, (devices, total), 0) * size
    own = ((r >= d) & (r < d + size)).astype(F32)
    r = lax.broadcasted_iota(jnp.int32, (1, total), 1).astype(F32)
    r = r - jnp.floor((r + 0.5) * (1.0 / size)) * size
    lane = lax.broadcasted_iota(jnp.int32, (LANES, total), 0).astype(F32)
    return own, (lane == r).astype(BF16)


def unpack_vectors(block):
    devices, unit, _ = block.shape

    def body(v_ref, out_ref, held):
        held[...] = v_ref[...].astype(F32)
        for size in (unit, 3 * unit, 4 * unit):
            own, lane = owner_masks(devices, size)
            for i in range(16):
                if sizes(unit)[i % 8] == size:
                    item = dot(held[:, i, :].astype(BF16), lane)
                    out_ref[i : i + 1, : devices * size] = jnp.sum(own * item, 0, keepdims=True)

    return launch(
        body,
        (block,),
        like((16, 4 * devices * unit), F32),
        scratch_shapes=[pltpu.VMEM(block.shape, F32)],
        name="unpack_vectors",
    )


def pack_gradients(sums, lift, boost, devices, after=()):
    unit = sums.shape[1] // devices
    shape = (devices, unit, LANES)

    def body(sums_ref, lift_ref, boost_ref, out_ref, held):
        held[...] = jnp.zeros_like(held)
        items = zip((GAIN, SHIFT, SCALE, CENTER, SETTLE), range(5))
        items = [(i, sums_ref[r : r + 1, :]) for i, r in items]
        for size, parts in (
            (unit, items),
            (3 * unit, [(LIFT, lift_ref[...])]),
            (4 * unit, [(BOOST, boost_ref[...])]),
        ):
            own, lane = owner_masks(devices, size)
            for i, value in parts:
                held[:, i, :] = dot_nt((own * value).astype(BF16), lane)
        out_ref[...] = held[...].astype(BF16)

    return launch(
        body,
        (sums, lift, boost),
        like(shape, BF16),
        after,
        scratch_shapes=[pltpu.VMEM(shape, F32)],
        name="pack_gradients",
    )


def flip(item, bit):
    return lax.ppermute(item, WIDE, [(i, i ^ bit) for i in range(8)])


def across_core(item):
    return flip(item, 1)


def across_x(item):
    return flip(item, 2)


def across_y(item):
    return flip(item, 4)


def along_z(item, step):
    return lax.ppermute(item, NARROW, [(i, (i + step) % 4) for i in range(4)])


def pack_shares(layers, matrices, unit):
    items = [row(layer[i]) for layer in layers for i in VECTORS]
    width = sum(m.shape[1] for m in matrices)
    count = len(matrices) + len(items)

    def body(*refs):
        mats, ins = refs[: len(matrices)], refs[len(matrices) : count]
        out_ref, held, sem, *parts = refs[count:]
        at, copies = 0, []
        for m in mats:
            target = out_ref.at[:, pl.ds(at, m.shape[1])]
            copies.append(pltpu.make_async_copy(m, target, sem.at[len(copies)]))
            at += m.shape[1]
        for item, part in zip(ins, parts):
            copies.append(pltpu.make_async_copy(item, part, sem.at[len(copies)]))
        for copy in copies:
            copy.start()
        held[...] = jnp.zeros_like(held)
        for copy in copies:
            copy.wait()
        for i, part in enumerate(parts):
            held[i : i + 1, : part.shape[1]] = part[...].astype(F32)
        out_ref[:, at:] = held[...].astype(BF16)

    return launch(
        body,
        [*matrices, *items],
        like((unit, width + LANES), BF16),
        in_specs=[ANY] * count,
        scratch_shapes=[pltpu.VMEM((unit, LANES), F32), pltpu.SemaphoreType.DMA((count,))]
        + [pltpu.VMEM(i.shape, BF16) for i in items],
        limit=60 * 1024 * 1024,
        name="pack_shares",
    )


def beside(items, unit, after=(), cover=SMALL):
    width = sum(i.shape[0] // unit * i.shape[1] for i in items)

    def body(*refs):
        out_ref, at = refs[-1], 0
        for item in refs[:-1]:
            for q in range(item.shape[0] // unit):
                out_ref[:, at : at + item.shape[1]] = item[q * unit : (q + 1) * unit, :]
                at += item.shape[1]

    return launch(
        body, items, like((unit, width), BF16), after, cover=cover, name="beside"
    )


class Gather:

    def __init__(self, share, where, widths):
        self.share, self.where, self.widths = share, where, widths
        self.ring = [share] + [along_z(share, k) for k in (1, 2, 3)]

    def stack(self, after=()):
        z = self.where[2]
        slots = jnp.stack([(z - k) % 4 for k in range(4)]).astype(jnp.int32)
        unit = self.share.shape[0]

        def body(slot_ref, *refs):
            items, outs = refs[:4], refs[4:]
            for i, item in enumerate(items):
                start = 0
                for out, width in zip(outs, self.widths):
                    out[slot_ref[i]] = item[:, start : start + width]
                    start += width

        outs = launch(
            body,
            (slots, *self.ring),
            [like((4, unit, w), BF16) for w in self.widths],
            after,
            in_specs=[SMEM] + [VMEM] * 4,
            name="stack_ring",
        )
        return [Plane(o, self.where) for o in outs]


class Plane:

    def __init__(self, own, where):
        self.own, self.where = own, where

    def near(self):
        self.sides = across_x(self.own), across_y(self.own)
        return self.sides

    def cut(self, after=()):
        shape = like((2,) + self.own.shape[1:], BF16)

        def body(left_ref, up_ref, up_out, left_out):
            up_out[...] = up_ref[:2]
            left_out[...] = left_ref[2:]

        self.halves = launch(body, self.sides, (shape, shape), after, name="cut")
        self.mine = (self.own, *self.sides)
        return self.halves

    def corner(self):
        self.halves, self.mine = fence(self.halves, self.mine)
        up, left = self.halves
        self.far = across_x(up), across_y(left)
        self.other = tuple(across_core(m) for m in self.mine)
        return self.far

    def assemble(self, widths, folds, after=()):
        plane, core, _ = self.where
        pieces = (*self.mine, *self.far, *self.other, *(across_core(f) for f in self.far))
        slots = jnp.stack(
            [(plane ^ r) * 2 + c for c in (core, 1 - core) for r in range(4)]
        ).astype(jnp.int32)
        unit = self.own.shape[1]

        def body(slot_ref, *refs):
            items, outs = refs[:10], refs[10:]
            for i, piece in enumerate(items):
                side, i = divmod(i, 5)
                slot = slot_ref[side * 4 + min(i, 3)]
                first = 2 if i == 4 else 0
                for z in range(piece.shape[0]):
                    start = 0
                    for out, width, fold in zip(outs, widths, folds):
                        part = width // fold
                        for q in range(fold):
                            cols = slice(start + q * part, start + (q + 1) * part)
                            if fold > 1:
                                out[slot, first + z, q] = piece[z, :, cols]
                            else:
                                out[slot, first + z] = piece[z, :, cols]
                        start += width

        outs = launch(
            body,
            (slots, *pieces),
            [
                like((8, 4, f, unit, w // f) if f > 1 else (8, 4, unit, w), BF16)
                for w, f in zip(widths, folds)
            ],
            after,
            in_specs=[SMEM] + [VMEM] * 10,
            name="assemble",
        )
        return [o.reshape(-1, o.shape[-1]) for o in outs]


def half_kernel(folds, tile, own, extra):
    count = len(folds)

    def body(index_ref, *refs):
        lefts, rights, refs = refs[:count], refs[count : 2 * count], refs[2 * count :]
        if extra:
            extra_ref, refs = refs[0], refs[1:]
        if own:
            arrived, refs = refs[0], refs[1:]
        keeps, outs = refs[-count:], refs[:-count]

        def emit(total, cols):
            if not own:
                outs[0][:, :, :, cols] = total.astype(BF16)
                return
            total = (total.astype(F32) + arrived[:, :, :, cols].astype(F32)).astype(BF16)
            p_ref, x_ref, y_ref, xp_ref, yp_ref = outs
            p_ref[:, :, cols] = total[0]
            x_ref[0, :, :, cols] = total[3, :2]
            x_ref[1, :, :, cols] = total[1, :2]
            xp_ref[:, :, cols] = total[1, 2:]
            y_ref[0, :, :, cols] = total[3, 2:]
            y_ref[1, :, :, cols] = total[2, 2:]
            yp_ref[:, :, cols] = total[2, :2]

        start = 0
        for left, right, keep, fold in zip(lefts, rights, keeps, folds):
            size = left.shape[0] // 8
            for r in range(4):
                at = pl.ds(pl.multiple_of(index_ref[r] * size, size), size)
                keep[r * size : (r + 1) * size, :] = left[at, :]
            width = right.shape[1]
            for j in range(0, width, tile):
                total = dot(keep[...], right[:, j : j + tile])
                total = total.reshape(4, 4, fold, size // 4 // fold, tile)
                for q in range(fold):
                    at = start + q * width + j
                    emit(total[:, :, q], slice(at, at + tile))
            start += fold * width
        if extra:
            total = jnp.stack([extra_ref[index_ref[r]] for r in range(4)])
            emit(total, slice(start, start + LANES))

    return body


class Scatter:

    def __init__(self, terms, extra, where):
        self.terms, self.extra, self.where = terms, extra, where
        self.unit = terms[0][0].shape[0] // 32 // terms[0][2]
        self.columns = sum(r.shape[1] * f for _, r, f in terms)
        self.columns += 0 if extra is None else LANES

    def half(self, core, arrived, after, tile=256):
        plane = self.where[0]
        index = jnp.stack([(plane ^ r) * 2 + core for r in range(4)]).astype(jnp.int32)
        lefts, rights, folds = zip(*self.terms)
        own = arrived is not None
        block = lambda *shape: like(shape + (self.unit, self.columns), BF16)
        if own:
            shapes = (block(4), block(2, 2), block(2, 2), block(2), block(2))
        else:
            shapes = block(4, 4)
        operands = [index, *lefts, *rights]
        if self.extra is not None:
            operands.append(self.extra.reshape(8, 4, self.unit, LANES))
        if own:
            operands.append(arrived)
        return launch(
            half_kernel(folds, tile, own, self.extra is not None),
            operands,
            shapes,
            after,
            in_specs=[SMEM] + [VMEM] * (len(operands) - 1),
            scratch_shapes=[pltpu.VMEM((l.shape[0] // 2, l.shape[1]), BF16) for l in lefts],
            name="own_half" if own else "other_half",
        )

    def other(self, after=()):
        out = self.half(1 - self.where[1], None, after)
        self.arrived = across_core(out)
        return out

    def own(self, after=()):
        self.p, x, y, self.xp, self.yp = self.half(self.where[1], self.arrived, after)
        self.x1, self.y1 = across_x(x), across_y(y)
        return self.p

    def far(self, after=()):
        shape = like(self.xp.shape, BF16)

        def body(xp_ref, y1_ref, yp_ref, x1_ref, x_ref, y_ref):
            x_ref[...] = (xp_ref[...].astype(F32) + y1_ref[0].astype(F32)).astype(BF16)
            y_ref[...] = (yp_ref[...].astype(F32) + x1_ref[0].astype(F32)).astype(BF16)

        operands = (self.xp, self.y1, self.yp, self.x1)
        xs, ys = launch(body, operands, (shape, shape), after, name="add_far")
        self.x2, self.y2 = across_x(xs), across_y(ys)
        return xs

    def near(self):
        return self.p, self.x1, self.y2, self.y1, self.x2


class Ring:

    def __init__(self, scatters):
        self.scatters = scatters
        self.unit = scatters[0].unit
        self.columns = sum(s.columns for s in scatters)

    def join(self, after=()):
        z = self.scatters[0].where[2]
        turn = jnp.stack([(z + k) % 4 for k in range(4)]).astype(jnp.int32)
        operands = [o for s in self.scatters for o in s.near()]
        widths = [s.columns for s in self.scatters]

        def body(turn_ref, *refs):
            ins, outs, held = refs[: len(operands)], refs[len(operands) : -1], refs[-1]
            start = 0
            for i, width in enumerate(widths):
                p_ref, x1_ref, y2_ref, y1_ref, x2_ref = ins[5 * i : 5 * i + 5]
                cols = slice(start, start + width)
                held[0:2, :, cols] = (
                    p_ref[0:2].astype(F32) + x1_ref[1].astype(F32) + y2_ref[...].astype(F32)
                )
                held[2:4, :, cols] = (
                    p_ref[2:4].astype(F32) + y1_ref[1].astype(F32) + x2_ref[...].astype(F32)
                )
                start += width
            for k, out in enumerate(outs):
                out[...] = held[turn_ref[k]].astype(BF16)

        blocks = launch(
            body,
            (turn, *operands),
            [like((self.unit, self.columns), BF16)] * 4,
            after,
            in_specs=[SMEM] + [VMEM] * len(operands),
            scratch_shapes=[pltpu.VMEM((4, self.unit, self.columns), F32)],
            name="join_plane",
        )
        self.got = [blocks[0]] + [along_z(blocks[k], k) for k in (1, 2, 3)]
        return blocks[0]

    def finish(self, widths, folds, vectors, after=(), cover=SMALL):
        unit = self.unit
        shapes = [like((f * unit, w), F32) for w, f in zip(widths, folds)]
        if vectors:
            shapes += [like((1, n), F32) for n in sizes(unit)]

        def body(*refs):
            ins, outs = refs[:4], refs[4:]

            def total(cols):
                return (
                    ins[0][:, cols].astype(F32)
                    + ins[1][:, cols].astype(F32)
                    + ins[2][:, cols].astype(F32)
                    + ins[3][:, cols].astype(F32)
                )

            start = 0
            for out, width, fold in zip(outs, widths, folds):
                for q in range(fold):
                    out[q * unit : (q + 1) * unit, :] = total(slice(start, start + width))
                    start += width
            if vectors:
                block = total(slice(start, start + LANES))
                for i, (out, n) in enumerate(zip(outs[len(widths) :], sizes(unit))):
                    out[...] = block[i : i + 1, :n]

        return launch(body, self.got, shapes, after, cover=cover, name="sum_ring")


def on_cube(stream, cotangent, segment_ids, *weights):
    one, two = weights[:12], weights[12:]
    unit = one[0].shape[0]
    count, length, width = stream.shape
    tokens = count * length
    hidden = 4 * width
    wide = lax.axis_index(WIDE)
    where = (wide // 2, wide % 2, lax.axis_index(NARROW))
    three = 3 * width
    h = stream.reshape(tokens, width)

    ISSUED.clear()
    head_share = pack_shares((one, two), [one[2], one[4]], unit)
    z_head = Gather(head_share, where, [4 * width + LANES])
    turns, mask = tables(segment_ids, width // HEADS)
    (h1,) = z_head.stack((turns, mask))
    near = h1.near()
    tail_share = beside([one[8], one[10]], unit, h1.own)
    z_tail = Gather(tail_share, where, [2 * hidden])
    head_two = beside([two[2], two[4]], unit, tail_share)
    tail_two = beside([two[8], two[10]], unit, head_two)
    h1.cut((tail_two, z_tail.ring[1:]))
    (t1,) = z_tail.stack(h1.halves)
    h1.halves, t1.own, head_two = fence(h1.halves, t1.own, head_two)
    corner = h1.corner()
    near = t1.near()
    z_two = Gather(head_two, where, [4 * width])
    packed, blend, block = h1.assemble((three, width, LANES), (1, 1, 1))
    vec = unpack_vectors(block.reshape(32, unit, LANES))
    first_t, q, k, v, att_t, base = run_attention_forward(0, h, vec, packed, blend, turns, mask)
    t1.cut((base, z_two.ring[1:]))
    (h2,) = z_two.stack(t1.halves)
    t1.halves, h2.own, tail_two = fence(t1.halves, h2.own, tail_two)
    corner = t1.corner()
    near = h2.near()
    z_last = Gather(tail_two, where, [hidden, hidden])
    widen, shrink = t1.assemble((hidden, hidden), (1, 4))
    second_t, active_t, slope = run_mlp_up(0, h, vec, widen)
    middle = run_mlp_down(0, active_t, shrink, vec, base, F32)
    saved = h, first_t, q, k, v, att_t, second_t, active_t, slope, packed, blend, widen, shrink
    h2.cut((middle, z_last.ring[1:]))
    w2, s2 = z_last.stack(h2.halves)
    h2.halves, w2.own = fence(h2.halves, w2.own)
    corner = h2.corner()
    near = w2.near()
    packed, blend = h2.assemble((three, width), (1, 1))
    first_t, q, k, v, att_t, base = run_attention_forward(
        1, middle, vec, packed, blend, turns, mask
    )
    w2.cut(base)
    w2.halves, s2.own = fence(w2.halves, s2.own)
    corner = w2.corner()
    near = s2.near()
    (widen,) = w2.assemble((hidden,), (1,))
    second_t, active_t, slope = run_mlp_up(1, middle, vec, widen)
    grad = low = cotangent.reshape(tokens, width)
    gs2 = Scatter([(active_t, low, 4)], None, where)
    token = gs2.other(active_t)
    s2.cut(token)
    corner = s2.corner()
    token = gs2.own(token)
    (shrink,) = s2.assemble((hidden,), (4,), token)

    up, g_boost, back = run_mlp_backward(low, shrink, widen, slope)
    gw2 = Scatter([(second_t, up, 1)], None, where)
    token = gw2.other(back)
    token = gs2.far((token, gs2.x1, gs2.y1))
    mixed, g_lift = run_attention_backward(low, blend, q, k, v, turns, mask, token)
    token = gw2.own((mixed, gw2.arrived, gs2.x2, gs2.y2))
    grad, low_one, sums = run_stream_backward(
        1, low, grad, middle, vec, back, packed, mixed, token
    )
    extra = pack_gradients(sums, g_lift, g_boost, 32)
    last = active_t, shrink, vec, base
    h, first_one, q, k, v, att_one, second_t, active_t, slope, packed, blend, widen, shrink = saved
    gp2 = Scatter(
        [(first_t, mixed, 1), (att_t, low, 1), (active_t, low_one, 4)], extra, where
    )
    token = gp2.other(extra)
    token = gw2.far((token, gw2.x1, gw2.y1))
    low = low_one
    up, g_boost, back = run_mlp_backward(low, shrink, widen, slope, token)
    gw1 = Scatter([(second_t, up, 1)], None, where)
    token = gw1.other(back)
    token = gp2.own((token, gp2.arrived, gw2.x2, gw2.y2))
    ring_two = Ring([gs2, gw2])
    token = ring_two.join(token)
    mixed, g_lift = run_attention_backward(low, blend, q, k, v, turns, mask, token)
    token = gw1.own((mixed, gw1.arrived))
    token = gp2.far((token, gp2.x1, gp2.y1))
    s_two, w_two = ring_two.finish((width, hidden), (4, 1), False, (token, ring_two.got))
    grad, _, sums = run_stream_backward(0, low, grad, h, vec, back, packed, mixed, s_two)
    extra = pack_gradients(sums, g_lift, g_boost, 32)
    gp1 = Scatter([(first_one, mixed, 1), (att_one, low, 1)], extra, where)
    token = gp1.other(extra)
    ring_mid = Ring([gp2])
    token = ring_mid.join((token, gp2.x2, gp2.y2))
    token = gw1.far((token, gw1.x1, gw1.y1))
    token = gp1.own((token, gp1.arrived))
    ending = run_mlp_down(1, *last, BF16, token)
    ring_one = Ring([gw1])
    token = ring_one.join((ending, gw1.x2, gw1.y2))
    token = gp1.far((token, gp1.x1, gp1.y1))
    p_two, b_two, s_one, *v_two = ring_mid.finish(
        (three, width, width), (1, 1, 4), True, (token, ring_mid.got), COVER
    )
    ring_end = Ring([gp1])
    token = ring_end.join((s_one, gp1.x2, gp1.y2))
    (w_one,) = ring_one.finish((hidden,), (1,), False, (token, ring_one.got), COVER)
    p_one, b_one, *v_one = ring_end.finish((three, width), (1, 1), True, (w_one, ring_end.got))

    out = []
    for p, b, w, s, v in (
        (p_one, b_one, w_one, s_one, v_one),
        (p_two, b_two, w_two, s_two, v_two),
    ):
        g = [None] * 12
        g[2], g[4], g[8], g[10] = p, b, w, s
        for i, item in zip(VECTORS, v):
            g[i] = item.reshape(-1)
        g[5] = g[11]
        out += g
    shape = (count, length, width)
    return (ending.reshape(shape), grad.reshape(shape)) + tuple(out)


def whole(item):
    return lax.all_gather(item, (WIDE, NARROW), axis=0, tiled=True)


def owned(item):
    for axis in (WIDE, NARROW):
        parts = lax.axis_size(axis)
        item = item.reshape((parts, item.shape[0] // parts) + item.shape[1:])
        item = lax.all_to_all(item.astype(BF16), axis, 0, 0, tiled=True)
        item = jnp.sum(item.astype(F32), 0)
    return item


def on_any(stream, cotangent, segment_ids, *weights):
    count, length, width = stream.shape
    tokens = count * length
    turns, mask = tables(segment_ids, width // HEADS)
    layers = [[whole(i) for i in layer] for layer in (weights[:12], weights[12:])]
    hidden = layers[0][9].shape[0]
    vec = [row(w[i]).astype(F32) for w in layers for i in VECTORS]
    vec = jnp.concatenate([jnp.pad(i, ((0, 0), (0, hidden - i.shape[1]))) for i in vec])
    h = stream.reshape(tokens, width)
    kept = []
    for l, w in enumerate(layers):
        packed, blend, widen, shrink = w[2], w[4], w[8], w[10]
        first_t, q, k, v, att_t, base = run_attention_forward(
            l, h, vec, packed, blend, turns, mask
        )
        second_t, active_t, slope = run_mlp_up(l, h, vec, widen)
        out = run_mlp_down(l, active_t, shrink, vec, base, F32)
        kept.append((h, first_t, q, k, v, att_t, second_t, active_t, slope))
        h = out
    result = h.astype(BF16).reshape(stream.shape)
    grad = low = cotangent.reshape(tokens, width)
    out = ()
    for l in (1, 0):
        h, first_t, q, k, v, att_t, second_t, active_t, slope = kept[l]
        packed, blend, widen, shrink = (layers[l][i] for i in (2, 4, 8, 10))
        up, g_boost, back = run_mlp_backward(low, shrink, widen, slope)
        mixed, g_lift = run_attention_backward(low, blend, q, k, v, turns, mask)
        grad, next_low, sums = run_stream_backward(l, low, grad, h, vec, back, packed, mixed)
        g_gain, g_shift, g_scale, g_center, g_settle = (owned(sums[i]) for i in range(5))
        out = (
            g_gain,
            g_shift,
            owned(dot(first_t, mixed)),
            owned(g_lift[0]),
            owned(dot(att_t, low)),
            g_settle,
            g_scale,
            g_center,
            owned(dot(second_t, up)),
            owned(g_boost[0]),
            owned(dot(active_t, low)),
            g_settle,
        ) + out
        low = next_low
    return (result, grad.reshape(stream.shape)) + out


def solution(mesh):
    axes = (WIDE, NARROW)
    one, two, three = P(axes), P(axes, None), P(axes, None, None)
    layer = (one, one, two, one, two, one, one, one, two, one, two, one)
    cube = dict(mesh.shape) == {WIDE: 8, NARROW: 4}
    return jax.shard_map(
        on_cube if cube else on_any,
        mesh=mesh,
        in_specs=(three, three, two) + layer + layer,
        out_specs=(three, three) + layer + layer,
        check_vma=False,
    )
```

```python
import jax
import jax.numpy as jnp
from jax import lax
from jax.experimental import pallas as pl
from jax.experimental.pallas import tpu as pltpu
from jax.sharding import PartitionSpec as P

HEADS = 12
ROT = 16
EPS = 1e-05
F32 = jnp.float32
BF16 = jnp.bfloat16
LANES = 128
COVER = 20
SMALL = 30
COVERS = {9: 5}
COSTS = {'attention_backward': 40, 'attention_forward': 40, 'mlp_up': 40, 'own_half': 3, 'other_half': 3, 'assemble': 1, 'unpack_vectors': 1}
COUNT = [0]
MASKED = -1000000000.0
VMEM_LIMIT = 24 * 1024 * 1024
WIDE, NARROW = "wide", "narrow"
SMEM = pl.BlockSpec(memory_space=pltpu.SMEM)
VMEM = pl.BlockSpec(memory_space=pltpu.VMEM)
ANY = pl.BlockSpec(memory_space=pl.ANY)
VECTORS = (0, 1, 3, 5, 6, 7, 9, 11)
GAIN, SHIFT, LIFT, NUDGE, SCALE, CENTER, BOOST, SETTLE = range(8)


def like(shape, kind):
    return jax.ShapeDtypeStruct(tuple(shape), kind)


def fence(*items):
    fenced = lax.optimization_barrier(items)
    for old, new in zip(jax.tree.leaves(items), jax.tree.leaves(fenced)):
        if id(old) in ISSUED:
            ISSUED[id(new)] = new, ISSUED[id(old)][1]
    return fenced


ISSUED = {}


def launch(
    body, operands, out_shape, after=(), in_specs=None, out_specs=None, cover=SMALL,
    limit=VMEM_LIMIT, **more
):
    micros = COVERS.get(COUNT[0], COSTS.get(more["name"], cover))
    COUNT[0] += 1
    operands = list(operands)
    several = isinstance(out_shape, (list, tuple))
    outs = list(out_shape) if several else [out_shape]
    if in_specs is None:
        in_specs = [VMEM] * len(operands)
    if out_specs is None:
        out_specs = [VMEM] * len(outs)
    elif not isinstance(out_specs, (list, tuple)):
        out_specs = [out_specs]
    waits, specs = [], []
    for item in jax.tree.leaves(after):
        small = ISSUED.get(id(item))
        small = (item, ANY) if small is None else (small[1], VMEM)
        if all(small[0] is not w for w in waits):
            waits.append(small[0])
            specs.append(small[1])
    count = len(operands)
    first = count + len(waits)
    grid = "grid" in more

    def kernel(*refs):
        end = first + len(outs)
        refs[end][...] = jnp.zeros_like(refs[end])
        body(*refs[:count], *refs[first:end], *refs[end + 1 :])

    signal = like((8, LANES), F32)
    whole = pl.BlockSpec((8, LANES), lambda j: (0, 0)) if grid else VMEM
    if grid:
        specs = [whole if s is VMEM else s for s in specs]
    results = pl.pallas_call(
        kernel,
        out_shape=(*outs, signal),
        in_specs=[*in_specs, *specs],
        out_specs=(*out_specs, whole),
        compiler_params=pltpu.CompilerParams(vmem_limit_bytes=limit),
        cost_estimate=pl.CostEstimate(
            flops=int(micros * 1e9), bytes_accessed=1000, transcendentals=0
        ),
        **more,
    )(*operands, *waits)
    for item in results[:-1]:
        ISSUED[id(item)] = item, results[-1]
    return results[:-1] if several else results[0]


def dot(left, right):
    return lax.dot_general(left, right, (((1,), (0,)), ((), ())), preferred_element_type=F32)


def dot_nt(left, right):
    return lax.dot_general(left, right, (((1,), (1,)), ((), ())), preferred_element_type=F32)


def dot_tn(left, right):
    return lax.dot_general(left, right, (((0,), (0,)), ((), ())), preferred_element_type=F32)


def tables(segments, head_size):
    length = segments.shape[-1]
    before = jnp.sum((segments[:, None, :] < segments[:, :, None]).astype(jnp.int32), -1)
    place = jnp.arange(length, dtype=jnp.int32)
    position = (place[None, :] - before).astype(F32).reshape(-1, 1)
    half = ROT // 2
    lane = jnp.arange(LANES, dtype=jnp.int32) % head_size
    freqs = 10000.0 ** (-((lane % half).astype(F32) * 2.0 / ROT))
    angle = position * freqs[None, :]
    lane = lane[None, :]
    cosine = jnp.where(lane < ROT, jnp.cos(angle), 1.0)
    sine = jnp.sin(angle)
    low = jnp.where(lane < half, -sine, 0.0)
    high = jnp.where((lane >= half) & (lane < ROT), sine, 0.0)
    allowed = (segments[:, :, None] == segments[:, None, :]) & (place[:, None] <= place[None, :])[
        None
    ]
    return jnp.stack([cosine, low, high]), jnp.where(allowed, 0.0, -1.0).astype(F32)


def whiten(x):
    centered = x - jnp.mean(x, -1, keepdims=True)
    spread = jnp.mean(centered * centered, -1, keepdims=True)
    scale = lax.rsqrt(spread + EPS)
    return centered * scale, scale


def vector(vec_ref, layer, which, cols):
    at = layer * 8 + which
    return vec_ref[at : at + 1, cols]


def lane_masks(head_size, value):
    lane = lax.broadcasted_iota(jnp.int32, (1, LANES), 1)
    return [
        jnp.where((lane >= i * head_size) & (lane < (i + 1) * head_size), value, 0.0).astype(BF16)
        for i in range(LANES // head_size)
    ]


def stacked(block, masks):
    return jnp.concatenate([block * m for m in masks], 0)


def softmax_halves(scores, masked):
    out = []
    for i in range(scores.shape[0] // LANES):
        logits = jnp.where(masked, MASKED, scores[i * LANES : (i + 1) * LANES])
        expo = jnp.exp(logits - jnp.max(logits, 0, keepdims=True))
        out.append(expo * (1.0 / jnp.sum(expo, 0, keepdims=True)))
    return out


def norm_rows(h_ref, vec_ref, layer, which, out_ref, out_t_ref):
    tokens, width = h_ref.shape
    cols = slice(0, width)

    @pl.loop(0, tokens // LANES)
    def _(r):
        at = pl.ds(pl.multiple_of(r * LANES, LANES), LANES)
        normed, _ = whiten(h_ref[at, :].astype(F32))
        item = normed * vector(vec_ref, layer, which, cols)
        item = (item + vector(vec_ref, layer, which + 1, cols)).astype(BF16)
        out_ref[at, :] = item
        out_t_ref[:, at] = item.T


def run_attention_forward(layer, h, vec, packed, blend, turns, mask, after=()):
    tokens, width = h.shape
    head_size = width // HEADS
    rows, length, _ = mask.shape

    def body(
        h_ref, vec_ref, packed_ref, blend_ref, turn_ref, mask_ref,
        first_t_ref, q_ref, k_ref, v_ref, att_t_ref, base_ref,
        first_ref, att_ref,
    ):
        norm_rows(h_ref, vec_ref, layer, GAIN, first_ref, first_t_ref)
        tile = 2 * LANES
        for j in range(width // tile):
            for part, out_ref in enumerate((q_ref, k_ref, v_ref)):
                cols = slice(part * width + j * tile, part * width + (j + 1) * tile)
                mixed = dot(first_ref[...], packed_ref[:, cols])
                mixed = mixed + vector(vec_ref, layer, LIFT, cols)
                for b in range(tile // LANES):
                    block = mixed[:, b * LANES : (b + 1) * LANES]
                    if part < 2:
                        block = (
                            block * turn_ref[0]
                            + pltpu.roll(block, LANES - ROT // 2, 1) * turn_ref[1]
                            + pltpu.roll(block, ROT // 2, 1) * turn_ref[2]
                        )
                    start = j * tile + b * LANES
                    out_ref[:, start : start + LANES] = block.astype(BF16)

        scaled = lane_masks(head_size, head_size ** (-0.5))
        plain = lane_masks(head_size, 1.0)

        @pl.loop(0, rows)
        def _(r):
            at = pl.ds(pl.multiple_of(r * length, length), length)
            masked = mask_ref[r] < 0.0
            for p in range(width // LANES):
                cols = slice(p * LANES, (p + 1) * LANES)
                scores = dot_nt(stacked(k_ref[at, cols], scaled), q_ref[at, cols])
                probs = [p.astype(BF16) for p in softmax_halves(scores, masked)]
                probs = jnp.concatenate(probs, 0)
                attended = dot_tn(probs, stacked(v_ref[at, cols], plain)).astype(BF16)
                att_ref[at, cols] = attended
                att_t_ref[cols, at] = attended.T

        for j in range(width // tile):
            cols = slice(j * tile, (j + 1) * tile)
            base_ref[:, cols] = (
                h_ref[:, cols].astype(F32)
                + dot(att_ref[...], blend_ref[:, cols])
                + vector(vec_ref, layer, NUDGE, cols)
            )

    square = like((tokens, width), BF16)
    turned = like((width, tokens), BF16)
    return launch(
        body,
        (h, vec, packed, blend, turns, mask),
        (turned, square, square, square, turned, like((tokens, width), F32)),
        after,
        scratch_shapes=[pltpu.VMEM((tokens, width), BF16)] * 2,
        cover=COVER,
        name="attention_forward",
    )


def gelu_pair(u):
    z = jnp.abs(u) * 0.7071067811865476
    t = 1.0 / (1.0 + 0.3275911 * z)
    poly = t * (
        0.127414796
        + t * (-0.142248368 + t * (0.7107068705 + t * (-0.7265760135 + t * 0.5307027145)))
    )
    bell = jnp.exp(-0.5 * u * u)
    tail = poly * bell
    cdf = jnp.where(u < 0.0, tail, 1.0 - tail)
    return u * cdf, cdf + u * bell * 0.3989422804014327


def run_mlp_up(layer, h, vec, widen, after=(), tile=512):
    tokens, width = h.shape
    hidden = widen.shape[1]

    def body(h_ref, vec_ref, widen_ref, second_t_ref, active_t_ref, slope_ref, second_ref):
        step = pl.program_id(0)

        @pl.when(step == 0)
        def _():
            norm_rows(h_ref, vec_ref, layer, SCALE, second_ref, second_t_ref)

        cols = pl.ds(pl.multiple_of(step * tile, tile), tile)
        upward = dot(second_ref[...], widen_ref[...]) + vector(vec_ref, layer, BOOST, cols)
        active, slope = gelu_pair(upward)
        slope_ref[...] = slope.astype(BF16)
        active_t_ref[...] = active.astype(BF16).T

    whole = lambda shape: pl.BlockSpec(shape, lambda j: (0, 0))
    return launch(
        body,
        (h, vec, widen),
        (like((width, tokens), BF16), like((hidden, tokens), BF16), like((tokens, hidden), BF16)),
        after,
        grid=(hidden // tile,),
        in_specs=[
            whole((tokens, width)),
            whole(vec.shape),
            pl.BlockSpec((width, tile), lambda j: (0, j)),
        ],
        out_specs=(
            whole((width, tokens)),
            pl.BlockSpec((tile, tokens), lambda j: (j, 0)),
            pl.BlockSpec((tokens, tile), lambda j: (0, j)),
        ),
        scratch_shapes=[pltpu.VMEM((tokens, width), BF16)],
        cover=COVER,
        name="mlp_up",
    )


def run_mlp_down(layer, active_t, shrink, vec, base, kind, after=()):
    def body(active_t_ref, shrink_ref, vec_ref, base_ref, out_ref):
        tile = 2 * LANES
        for j in range(out_ref.shape[1] // tile):
            cols = slice(j * tile, (j + 1) * tile)
            total = dot_tn(active_t_ref[...], shrink_ref[:, cols])
            total = total + vector(vec_ref, layer, SETTLE, cols)
            out_ref[:, cols] = (base_ref[:, cols] + total).astype(out_ref.dtype)

    return launch(
        body, (active_t, shrink, vec, base), like(base.shape, kind), after, cover=COVER, name="mlp_down"
    )


def run_mlp_backward(grad, shrink, widen, slope, after=(), tile=512):
    tokens, width = grad.shape
    hidden = widen.shape[1]

    def body(grad_ref, shrink_ref, widen_ref, slope_ref, up_ref, boost_ref, second_ref):
        step = pl.program_id(0)
        active = dot_nt(grad_ref[...], shrink_ref[...])
        up = (active * slope_ref[...].astype(F32)).astype(BF16)
        up_ref[...] = up
        boost_ref[...] = jnp.sum(up.astype(F32), 0, keepdims=True)
        back = dot_nt(up, widen_ref[...])

        @pl.when(step == 0)
        def _():
            second_ref[...] = back

        @pl.when(step > 0)
        def _():
            second_ref[...] += back

    whole = lambda shape: pl.BlockSpec(shape, lambda j: (0, 0))
    return launch(
        body,
        (grad, shrink, widen, slope),
        (like((tokens, hidden), BF16), like((1, hidden), F32), like((tokens, width), F32)),
        after,
        grid=(hidden // tile,),
        in_specs=[
            whole((tokens, width)),
            pl.BlockSpec((tile, width), lambda j: (j, 0)),
            pl.BlockSpec((width, tile), lambda j: (0, j)),
            pl.BlockSpec((tokens, tile), lambda j: (0, j)),
        ],
        out_specs=(
            pl.BlockSpec((tokens, tile), lambda j: (0, j)),
            pl.BlockSpec((1, tile), lambda j: (0, j)),
            whole((tokens, width)),
        ),
        cover=COVER,
        name="mlp_backward",
    )


def run_attention_backward(grad, blend, q, k, v, turns, mask, after=()):
    tokens, width = grad.shape
    head_size = width // HEADS
    rows, length, _ = mask.shape

    def body(
        grad_ref, blend_ref, q_ref, k_ref, v_ref, turn_ref, mask_ref, mixed_ref, lift_ref, datt_ref
    ):
        tile = 2 * LANES
        for j in range(width // tile):
            cols = slice(j * tile, (j + 1) * tile)
            datt_ref[:, cols] = dot_nt(grad_ref[...], blend_ref[cols, :]).astype(BF16)

        scaled = lane_masks(head_size, head_size ** (-0.5))
        plain = lane_masks(head_size, 1.0)

        @pl.loop(0, rows)
        def _(r):
            at = pl.ds(pl.multiple_of(r * length, length), length)
            masked = mask_ref[r] < 0.0
            cos, low, high = turn_ref[0, at, :], turn_ref[1, at, :], turn_ref[2, at, :]

            def unturn(block):
                return (
                    block * cos
                    + pltpu.roll(block * low, ROT // 2, 1)
                    + pltpu.roll(block * high, LANES - ROT // 2, 1)
                )

            lane = lax.broadcasted_iota(jnp.int32, (length, LANES), 1)
            for p in range(width // LANES):
                cols = slice(p * LANES, (p + 1) * LANES)
                query, values, datt = q_ref[at, cols], v_ref[at, cols], datt_ref[at, cols]
                keys = stacked(k_ref[at, cols], scaled)
                probs = softmax_halves(dot_nt(keys, query), masked)
                dprobs = dot_nt(stacked(values, plain), datt)
                draw = []
                for i, prob in enumerate(probs):
                    dprob = dprobs[i * LANES : (i + 1) * LANES]
                    inner = jnp.sum(prob * dprob, 0, keepdims=True)
                    draw.append((prob * (dprob - inner)).astype(BF16))
                draw = jnp.concatenate(draw, 0)
                low_probs = jnp.concatenate([x.astype(BF16) for x in probs], 0)
                dvalues = dot(low_probs, datt)
                dkeys = dot(draw, query)
                dquery = dot_tn(draw, keys)
                dvalues = jnp.where(lane < head_size, dvalues[:length], dvalues[length:])
                dkeys = jnp.where(lane < head_size, dkeys[:length], dkeys[length:])
                dkeys = dkeys * (head_size ** (-0.5))
                for part, item in enumerate((unturn(dquery), unturn(dkeys), dvalues)):
                    start = part * width + p * LANES
                    mixed_ref[at, start : start + LANES] = item.astype(BF16)

        for j in range(3 * width // tile):
            cols = slice(j * tile, (j + 1) * tile)
            lift_ref[:, cols] = jnp.sum(mixed_ref[:, cols].astype(F32), 0, keepdims=True)

    return launch(
        body,
        (grad, blend, q, k, v, turns, mask),
        (like((tokens, 3 * width), BF16), like((1, 3 * width), F32)),
        after,
        scratch_shapes=[pltpu.VMEM((tokens, width), BF16)],
        cover=COVER,
        name="attention_backward",
    )


def run_stream_backward(layer, grad, out_grad, h, vec, second, packed, mixed, after=()):
    tokens, width = grad.shape

    def body(
        grad_ref, out_grad_ref, h_ref, vec_ref, second_ref, packed_ref, mixed_ref,
        in_grad_ref, low_ref, sums_ref,
        dfirst_ref,
    ):
        tile = 2 * LANES
        for j in range(width // tile):
            cols = slice(j * tile, (j + 1) * tile)
            dfirst_ref[:, cols] = dot_nt(mixed_ref[...], packed_ref[cols, :])
        sums_ref[...] = jnp.zeros_like(sums_ref)
        cols = slice(0, width)

        @pl.loop(0, tokens // LANES)
        def _(r):
            at = pl.ds(pl.multiple_of(r * LANES, LANES), LANES)
            normed, spread = whiten(h_ref[at, :].astype(F32))
            first, second = dfirst_ref[at, :], second_ref[at, :]
            low_grad = grad_ref[at, :].astype(F32)
            for i, item in enumerate((first * normed, first, second * normed, second, low_grad)):
                sums_ref[i : i + 1, :] += jnp.sum(item, 0, keepdims=True)
            inner = first * vector(vec_ref, layer, GAIN, cols)
            inner = inner + second * vector(vec_ref, layer, SCALE, cols)
            along = jnp.mean(inner * normed, -1, keepdims=True)
            inner = inner - jnp.mean(inner, -1, keepdims=True) - normed * along
            total = out_grad_ref[at, :].astype(F32) + inner * spread
            in_grad_ref[at, :] = total
            low_ref[at, :] = total.astype(BF16)

    return launch(
        body,
        (grad, out_grad, h, vec, second, packed, mixed),
        (like((tokens, width), F32), like((tokens, width), BF16), like((8, width), F32)),
        after,
        scratch_shapes=[pltpu.VMEM((tokens, width), F32)],
        cover=COVER,
        name="stream_backward",
    )


def sizes(unit):
    return (unit, unit, 3 * unit, unit, unit, unit, 4 * unit, unit)


def row(item):
    return item.reshape(1, -1)


def owner_masks(devices, size):
    total = devices * size
    r = lax.broadcasted_iota(jnp.int32, (devices, total), 1)
    d = lax.broadcasted_iota(jnp.int32, (devices, total), 0) * size
    own = ((r >= d) & (r < d + size)).astype(F32)
    r = lax.broadcasted_iota(jnp.int32, (1, total), 1).astype(F32)
    r = r - jnp.floor((r + 0.5) * (1.0 / size)) * size
    lane = lax.broadcasted_iota(jnp.int32, (LANES, total), 0).astype(F32)
    return own, (lane == r).astype(BF16)


def unpack_vectors(block):
    devices, unit, _ = block.shape

    def body(v_ref, out_ref, held):
        held[...] = v_ref[...].astype(F32)
        for size in (unit, 3 * unit, 4 * unit):
            own, lane = owner_masks(devices, size)
            for i in range(16):
                if sizes(unit)[i % 8] == size:
                    item = dot(held[:, i, :].astype(BF16), lane)
                    out_ref[i : i + 1, : devices * size] = jnp.sum(own * item, 0, keepdims=True)

    return launch(
        body,
        (block,),
        like((16, 4 * devices * unit), F32),
        scratch_shapes=[pltpu.VMEM(block.shape, F32)],
        name="unpack_vectors",
    )


def pack_gradients(sums, lift, boost, devices, after=()):
    unit = sums.shape[1] // devices
    shape = (devices, unit, LANES)

    def body(sums_ref, lift_ref, boost_ref, out_ref, held):
        held[...] = jnp.zeros_like(held)
        items = zip((GAIN, SHIFT, SCALE, CENTER, SETTLE), range(5))
        items = [(i, sums_ref[r : r + 1, :]) for i, r in items]
        for size, parts in (
            (unit, items),
            (3 * unit, [(LIFT, lift_ref[...])]),
            (4 * unit, [(BOOST, boost_ref[...])]),
        ):
            own, lane = owner_masks(devices, size)
            for i, value in parts:
                held[:, i, :] = dot_nt((own * value).astype(BF16), lane)
        out_ref[...] = held[...].astype(BF16)

    return launch(
        body,
        (sums, lift, boost),
        like(shape, BF16),
        after,
        scratch_shapes=[pltpu.VMEM(shape, F32)],
        name="pack_gradients",
    )


def flip(item, bit):
    return lax.ppermute(item, WIDE, [(i, i ^ bit) for i in range(8)])


def across_core(item):
    return flip(item, 1)


def across_x(item):
    return flip(item, 2)


def across_y(item):
    return flip(item, 4)


def along_z(item, step):
    return lax.ppermute(item, NARROW, [(i, (i + step) % 4) for i in range(4)])


def pack_shares(layers, matrices, unit):
    items = [row(layer[i]) for layer in layers for i in VECTORS]
    width = sum(m.shape[1] for m in matrices)
    count = len(matrices) + len(items)

    def body(*refs):
        mats, ins = refs[: len(matrices)], refs[len(matrices) : count]
        out_ref, held, sem, *parts = refs[count:]
        at, copies = 0, []
        for m in mats:
            target = out_ref.at[:, pl.ds(at, m.shape[1])]
            copies.append(pltpu.make_async_copy(m, target, sem.at[len(copies)]))
            at += m.shape[1]
        for item, part in zip(ins, parts):
            copies.append(pltpu.make_async_copy(item, part, sem.at[len(copies)]))
        for copy in copies:
            copy.start()
        held[...] = jnp.zeros_like(held)
        for copy in copies:
            copy.wait()
        for i, part in enumerate(parts):
            held[i : i + 1, : part.shape[1]] = part[...].astype(F32)
        out_ref[:, at:] = held[...].astype(BF16)

    return launch(
        body,
        [*matrices, *items],
        like((unit, width + LANES), BF16),
        in_specs=[ANY] * count,
        scratch_shapes=[pltpu.VMEM((unit, LANES), F32), pltpu.SemaphoreType.DMA((count,))]
        + [pltpu.VMEM(i.shape, BF16) for i in items],
        limit=60 * 1024 * 1024,
        name="pack_shares",
    )


def beside(items, unit, after=(), cover=SMALL):
    width = sum(i.shape[0] // unit * i.shape[1] for i in items)

    def body(*refs):
        out_ref, at = refs[-1], 0
        for item in refs[:-1]:
            for q in range(item.shape[0] // unit):
                out_ref[:, at : at + item.shape[1]] = item[q * unit : (q + 1) * unit, :]
                at += item.shape[1]

    return launch(
        body, items, like((unit, width), BF16), after, cover=cover, name="beside"
    )


class Gather:

    def __init__(self, share, where, widths):
        self.share, self.where, self.widths = share, where, widths
        self.ring = [share] + [along_z(share, k) for k in (1, 2, 3)]

    def stack(self, after=()):
        z = self.where[2]
        slots = jnp.stack([(z - k) % 4 for k in range(4)]).astype(jnp.int32)
        unit = self.share.shape[0]

        def body(slot_ref, *refs):
            items, outs = refs[:4], refs[4:]
            for i, item in enumerate(items):
                start = 0
                for out, width in zip(outs, self.widths):
                    out[slot_ref[i]] = item[:, start : start + width]
                    start += width

        outs = launch(
            body,
            (slots, *self.ring),
            [like((4, unit, w), BF16) for w in self.widths],
            after,
            in_specs=[SMEM] + [VMEM] * 4,
            name="stack_ring",
        )
        return [Plane(o, self.where) for o in outs]


class Plane:

    def __init__(self, own, where):
        self.own, self.where = own, where

    def near(self):
        self.sides = across_x(self.own), across_y(self.own)
        return self.sides

    def cut(self, after=()):
        shape = like((2,) + self.own.shape[1:], BF16)

        def body(left_ref, up_ref, up_out, left_out):
            up_out[...] = up_ref[:2]
            left_out[...] = left_ref[2:]

        self.halves = launch(body, self.sides, (shape, shape), after, name="cut")
        self.mine = (self.own, *self.sides)
        return self.halves

    def corner(self):
        self.halves, self.mine = fence(self.halves, self.mine)
        up, left = self.halves
        self.far = across_x(up), across_y(left)
        self.other = tuple(across_core(m) for m in self.mine)
        return self.far

    def assemble(self, widths, folds, after=()):
        plane, core, _ = self.where
        pieces = (*self.mine, *self.far, *self.other, *(across_core(f) for f in self.far))
        slots = jnp.stack(
            [(plane ^ r) * 2 + c for c in (core, 1 - core) for r in range(4)]
        ).astype(jnp.int32)
        unit = self.own.shape[1]

        def body(slot_ref, *refs):
            items, outs = refs[:10], refs[10:]
            for i, piece in enumerate(items):
                side, i = divmod(i, 5)
                slot = slot_ref[side * 4 + min(i, 3)]
                first = 2 if i == 4 else 0
                for z in range(piece.shape[0]):
                    start = 0
                    for out, width, fold in zip(outs, widths, folds):
                        part = width // fold
                        for q in range(fold):
                            cols = slice(start + q * part, start + (q + 1) * part)
                            if fold > 1:
                                out[slot, first + z, q] = piece[z, :, cols]
                            else:
                                out[slot, first + z] = piece[z, :, cols]
                        start += width

        outs = launch(
            body,
            (slots, *pieces),
            [
                like((8, 4, f, unit, w // f) if f > 1 else (8, 4, unit, w), BF16)
                for w, f in zip(widths, folds)
            ],
            after,
            in_specs=[SMEM] + [VMEM] * 10,
            name="assemble",
        )
        return [o.reshape(-1, o.shape[-1]) for o in outs]


def half_kernel(folds, tile, own, extra):
    count = len(folds)

    def body(index_ref, *refs):
        lefts, rights, refs = refs[:count], refs[count : 2 * count], refs[2 * count :]
        if extra:
            extra_ref, refs = refs[0], refs[1:]
        if own:
            arrived, refs = refs[0], refs[1:]
        keeps, outs = refs[-count:], refs[:-count]

        def emit(total, cols):
            if not own:
                outs[0][:, :, :, cols] = total.astype(BF16)
                return
            total = (total.astype(F32) + arrived[:, :, :, cols].astype(F32)).astype(BF16)
            p_ref, x_ref, y_ref, xp_ref, yp_ref = outs
            p_ref[:, :, cols] = total[0]
            x_ref[0, :, :, cols] = total[3, :2]
            x_ref[1, :, :, cols] = total[1, :2]
            xp_ref[:, :, cols] = total[1, 2:]
            y_ref[0, :, :, cols] = total[3, 2:]
            y_ref[1, :, :, cols] = total[2, 2:]
            yp_ref[:, :, cols] = total[2, :2]

        start = 0
        for left, right, keep, fold in zip(lefts, rights, keeps, folds):
            size = left.shape[0] // 8
            for r in range(4):
                at = pl.ds(pl.multiple_of(index_ref[r] * size, size), size)
                keep[r * size : (r + 1) * size, :] = left[at, :]
            width = right.shape[1]
            for j in range(0, width, tile):
                total = dot(keep[...], right[:, j : j + tile])
                total = total.reshape(4, 4, fold, size // 4 // fold, tile)
                for q in range(fold):
                    at = start + q * width + j
                    emit(total[:, :, q], slice(at, at + tile))
            start += fold * width
        if extra:
            total = jnp.stack([extra_ref[index_ref[r]] for r in range(4)])
            emit(total, slice(start, start + LANES))

    return body


class Scatter:

    def __init__(self, terms, extra, where):
        self.terms, self.extra, self.where = terms, extra, where
        self.unit = terms[0][0].shape[0] // 32 // terms[0][2]
        self.columns = sum(r.shape[1] * f for _, r, f in terms)
        self.columns += 0 if extra is None else LANES

    def half(self, core, arrived, after, tile=256):
        plane = self.where[0]
        index = jnp.stack([(plane ^ r) * 2 + core for r in range(4)]).astype(jnp.int32)
        lefts, rights, folds = zip(*self.terms)
        own = arrived is not None
        block = lambda *shape: like(shape + (self.unit, self.columns), BF16)
        if own:
            shapes = (block(4), block(2, 2), block(2, 2), block(2), block(2))
        else:
            shapes = block(4, 4)
        operands = [index, *lefts, *rights]
        if self.extra is not None:
            operands.append(self.extra.reshape(8, 4, self.unit, LANES))
        if own:
            operands.append(arrived)
        return launch(
            half_kernel(folds, tile, own, self.extra is not None),
            operands,
            shapes,
            after,
            in_specs=[SMEM] + [VMEM] * (len(operands) - 1),
            scratch_shapes=[pltpu.VMEM((l.shape[0] // 2, l.shape[1]), BF16) for l in lefts],
            name="own_half" if own else "other_half",
        )

    def other(self, after=()):
        out = self.half(1 - self.where[1], None, after)
        self.arrived = across_core(out)
        return out

    def own(self, after=()):
        self.p, x, y, self.xp, self.yp = self.half(self.where[1], self.arrived, after)
        self.x1, self.y1 = across_x(x), across_y(y)
        return self.p

    def far(self, after=()):
        shape = like(self.xp.shape, BF16)

        def body(xp_ref, y1_ref, yp_ref, x1_ref, x_ref, y_ref):
            x_ref[...] = (xp_ref[...].astype(F32) + y1_ref[0].astype(F32)).astype(BF16)
            y_ref[...] = (yp_ref[...].astype(F32) + x1_ref[0].astype(F32)).astype(BF16)

        operands = (self.xp, self.y1, self.yp, self.x1)
        xs, ys = launch(body, operands, (shape, shape), after, name="add_far")
        self.x2, self.y2 = across_x(xs), across_y(ys)
        return xs

    def near(self):
        return self.p, self.x1, self.y2, self.y1, self.x2


class Ring:

    def __init__(self, scatters):
        self.scatters = scatters
        self.unit = scatters[0].unit
        self.columns = sum(s.columns for s in scatters)

    def join(self, after=()):
        z = self.scatters[0].where[2]
        turn = jnp.stack([(z + k) % 4 for k in range(4)]).astype(jnp.int32)
        operands = [o for s in self.scatters for o in s.near()]
        widths = [s.columns for s in self.scatters]

        def body(turn_ref, *refs):
            ins, outs, held = refs[: len(operands)], refs[len(operands) : -1], refs[-1]
            start = 0
            for i, width in enumerate(widths):
                p_ref, x1_ref, y2_ref, y1_ref, x2_ref = ins[5 * i : 5 * i + 5]
                cols = slice(start, start + width)
                held[0:2, :, cols] = (
                    p_ref[0:2].astype(F32) + x1_ref[1].astype(F32) + y2_ref[...].astype(F32)
                )
                held[2:4, :, cols] = (
                    p_ref[2:4].astype(F32) + y1_ref[1].astype(F32) + x2_ref[...].astype(F32)
                )
                start += width
            for k, out in enumerate(outs):
                out[...] = held[turn_ref[k]].astype(BF16)

        blocks = launch(
            body,
            (turn, *operands),
            [like((self.unit, self.columns), BF16)] * 4,
            after,
            in_specs=[SMEM] + [VMEM] * len(operands),
            scratch_shapes=[pltpu.VMEM((4, self.unit, self.columns), F32)],
            name="join_plane",
        )
        self.got = [blocks[0]] + [along_z(blocks[k], k) for k in (1, 2, 3)]
        return blocks[0]

    def finish(self, widths, folds, vectors, after=(), cover=SMALL):
        unit = self.unit
        shapes = [like((f * unit, w), F32) for w, f in zip(widths, folds)]
        if vectors:
            shapes += [like((1, n), F32) for n in sizes(unit)]

        def body(*refs):
            ins, outs = refs[:4], refs[4:]

            def total(cols):
                return (
                    ins[0][:, cols].astype(F32)
                    + ins[1][:, cols].astype(F32)
                    + ins[2][:, cols].astype(F32)
                    + ins[3][:, cols].astype(F32)
                )

            start = 0
            for out, width, fold in zip(outs, widths, folds):
                for q in range(fold):
                    out[q * unit : (q + 1) * unit, :] = total(slice(start, start + width))
                    start += width
            if vectors:
                block = total(slice(start, start + LANES))
                for i, (out, n) in enumerate(zip(outs[len(widths) :], sizes(unit))):
                    out[...] = block[i : i + 1, :n]

        return launch(body, self.got, shapes, after, cover=cover, name="sum_ring")


def on_cube(stream, cotangent, segment_ids, *weights):
    one, two = weights[:12], weights[12:]
    unit = one[0].shape[0]
    count, length, width = stream.shape
    tokens = count * length
    hidden = 4 * width
    wide = lax.axis_index(WIDE)
    where = (wide // 2, wide % 2, lax.axis_index(NARROW))
    three = 3 * width
    h = stream.reshape(tokens, width)

    ISSUED.clear()
    COUNT[0] = 0
    head_share = pack_shares((one, two), [one[2], one[4]], unit)
    z_head = Gather(head_share, where, [4 * width + LANES])
    tail_share = beside([one[8], one[10]], unit, head_share)
    z_tail = Gather(tail_share, where, [2 * hidden])
    turns, mask = tables(segment_ids, width // HEADS)
    (h1,) = z_head.stack((turns, mask))
    near = h1.near()
    head_two = beside([two[2], two[4]], unit, (tail_share, h1.own))
    tail_two = beside([two[8], two[10]], unit, head_two)
    h1.cut((tail_two, z_tail.ring[1:]))
    (t1,) = z_tail.stack(h1.halves)
    h1.halves, t1.own, head_two = fence(h1.halves, t1.own, head_two)
    corner = h1.corner()
    near = t1.near()
    z_two = Gather(head_two, where, [4 * width])
    packed, blend, block = h1.assemble((three, width, LANES), (1, 1, 1))
    vec = unpack_vectors(block.reshape(32, unit, LANES))
    first_t, q, k, v, att_t, base = run_attention_forward(0, h, vec, packed, blend, turns, mask)
    t1.cut((base, z_two.ring[1:]))
    (h2,) = z_two.stack(t1.halves)
    t1.halves, h2.own, tail_two = fence(t1.halves, h2.own, tail_two)
    corner = t1.corner()
    near = h2.near()
    z_last = Gather(tail_two, where, [hidden, hidden])
    widen, shrink = t1.assemble((hidden, hidden), (1, 4))
    second_t, active_t, slope = run_mlp_up(0, h, vec, widen)
    h2.cut(active_t)
    middle = run_mlp_down(0, active_t, shrink, vec, base, F32)
    saved = h, first_t, q, k, v, att_t, second_t, active_t, slope, packed, blend, widen, shrink
    w2, s2 = z_last.stack((h2.halves, middle))
    corner = h2.corner()
    near = w2.near()
    packed, blend = h2.assemble((three, width), (1, 1))
    first_t, q, k, v, att_t, base = run_attention_forward(
        1, middle, vec, packed, blend, turns, mask
    )
    w2.cut(base)
    w2.halves, s2.own = fence(w2.halves, s2.own)
    corner = w2.corner()
    near = s2.near()
    (widen,) = w2.assemble((hidden,), (1,))
    second_t, active_t, slope = run_mlp_up(1, middle, vec, widen)
    grad = low = cotangent.reshape(tokens, width)
    gs2 = Scatter([(active_t, low, 4)], None, where)
    token = gs2.other(active_t)
    s2.cut(token)
    s2.corner()
    token = gs2.own(token)
    (shrink,) = s2.assemble((hidden,), (4,), token)

    up, g_boost, back = run_mlp_backward(low, shrink, widen, slope)
    gw2 = Scatter([(second_t, up, 1)], None, where)
    token = gw2.other(back)
    token = gs2.far((token, gs2.x1, gs2.y1))
    mixed, g_lift = run_attention_backward(low, blend, q, k, v, turns, mask, token)
    token = gw2.own((mixed, gs2.x2, gs2.y2))
    grad, low_one, sums = run_stream_backward(
        1, low, grad, middle, vec, back, packed, mixed, token
    )
    extra = pack_gradients(sums, g_lift, g_boost, 32)
    last = active_t, shrink, vec, base
    h, first_one, q, k, v, att_one, second_t, active_t, slope, packed, blend, widen, shrink = saved
    gp2 = Scatter([(first_t, mixed, 1), (att_t, low, 1)], extra, where)
    token = gp2.other(extra)
    token = gw2.far(token)
    low = low_one
    up, g_boost, back = run_mlp_backward(low, shrink, widen, slope, token)
    gm1 = Scatter([(active_t, low, 4), (second_t, up, 1)], None, where)
    token = gp2.own((back, gw2.x2, gw2.y2))
    token = gm1.other(token)
    ring_two = Ring([gs2, gw2])
    token = ring_two.join(token)
    mixed, g_lift = run_attention_backward(low, blend, q, k, v, turns, mask, token)
    token = gp2.far(mixed)
    token = gm1.own(token)
    s_two, w_two = ring_two.finish((width, hidden), (4, 1), False, token)
    token = s_two
    grad, _, sums = run_stream_backward(0, low, grad, h, vec, back, packed, mixed, token)
    extra = pack_gradients(sums, g_lift, g_boost, 32)
    gp1 = Scatter([(first_one, mixed, 1), (att_one, low, 1)], extra, where)
    token = gp1.other(extra)
    ring_two_p, ring_one, ring_end = Ring([gp2]), Ring([gm1]), Ring([gp1])
    token = ring_two_p.join(token)
    token = gp1.own(token)
    token = gm1.far(token)
    token = ending = run_mlp_down(1, *last, BF16, token)
    p_two, b_two, *v_two = ring_two_p.finish((three, width), (1, 1), True, token)
    token = gp1.far(p_two)
    token = ring_one.join(token)
    token = ring_end.join(token)
    s_one, w_one = ring_one.finish((width, hidden), (4, 1), False, token)
    p_one, b_one, *v_one = ring_end.finish((three, width), (1, 1), True, w_one)

    out = []
    for p, b, w, s, v in (
        (p_one, b_one, w_one, s_one, v_one),
        (p_two, b_two, w_two, s_two, v_two),
    ):
        g = [None] * 12
        g[2], g[4], g[8], g[10] = p, b, w, s
        for i, item in zip(VECTORS, v):
            g[i] = item.reshape(-1)
        g[5] = g[11]
        out += g
    shape = (count, length, width)
    return (ending.reshape(shape), grad.reshape(shape)) + tuple(out)


def whole(item):
    return lax.all_gather(item, (WIDE, NARROW), axis=0, tiled=True)


def owned(item):
    for axis in (WIDE, NARROW):
        parts = lax.axis_size(axis)
        item = item.reshape((parts, item.shape[0] // parts) + item.shape[1:])
        item = lax.all_to_all(item.astype(BF16), axis, 0, 0, tiled=True)
        item = jnp.sum(item.astype(F32), 0)
    return item


def on_any(stream, cotangent, segment_ids, *weights):
    count, length, width = stream.shape
    tokens = count * length
    turns, mask = tables(segment_ids, width // HEADS)
    layers = [[whole(i) for i in layer] for layer in (weights[:12], weights[12:])]
    hidden = layers[0][9].shape[0]
    vec = [row(w[i]).astype(F32) for w in layers for i in VECTORS]
    vec = jnp.concatenate([jnp.pad(i, ((0, 0), (0, hidden - i.shape[1]))) for i in vec])
    h = stream.reshape(tokens, width)
    kept = []
    for l, w in enumerate(layers):
        packed, blend, widen, shrink = w[2], w[4], w[8], w[10]
        first_t, q, k, v, att_t, base = run_attention_forward(
            l, h, vec, packed, blend, turns, mask
        )
        second_t, active_t, slope = run_mlp_up(l, h, vec, widen)
        out = run_mlp_down(l, active_t, shrink, vec, base, F32)
        kept.append((h, first_t, q, k, v, att_t, second_t, active_t, slope))
        h = out
    result = h.astype(BF16).reshape(stream.shape)
    grad = low = cotangent.reshape(tokens, width)
    out = ()
    for l in (1, 0):
        h, first_t, q, k, v, att_t, second_t, active_t, slope = kept[l]
        packed, blend, widen, shrink = (layers[l][i] for i in (2, 4, 8, 10))
        up, g_boost, back = run_mlp_backward(low, shrink, widen, slope)
        mixed, g_lift = run_attention_backward(low, blend, q, k, v, turns, mask)
        grad, next_low, sums = run_stream_backward(l, low, grad, h, vec, back, packed, mixed)
        g_gain, g_shift, g_scale, g_center, g_settle = (owned(sums[i]) for i in range(5))
        out = (
            g_gain,
            g_shift,
            owned(dot(first_t, mixed)),
            owned(g_lift[0]),
            owned(dot(att_t, low)),
            g_settle,
            g_scale,
            g_center,
            owned(dot(second_t, up)),
            owned(g_boost[0]),
            owned(dot(active_t, low)),
            g_settle,
        ) + out
        low = next_low
    return (result, grad.reshape(stream.shape)) + out


def solution(mesh):
    axes = (WIDE, NARROW)
    one, two, three = P(axes), P(axes, None), P(axes, None, None)
    layer = (one, one, two, one, two, one, one, one, two, one, two, one)
    cube = dict(mesh.shape) == {WIDE: 8, NARROW: 4}
    return jax.shard_map(
        on_cube if cube else on_any,
        mesh=mesh,
        in_specs=(three, three, two) + layer + layer,
        out_specs=(three, three) + layer + layer,
        check_vma=False,
    )
```

```python
import jax
import jax.numpy as jnp
from jax import lax
from jax.experimental import pallas as pl
from jax.experimental.pallas import tpu as pltpu
from jax.sharding import PartitionSpec as P

HEADS = 12
ROT = 16
EPS = 1e-05
F32 = jnp.float32
BF16 = jnp.bfloat16
LANES = 128
COVER = 20
SMALL = 30
COVERS = {9: 5, 31: 40, 43: 40, 48: 1}
COSTS = {'attention_backward': 40, 'attention_forward': 40, 'mlp_up': 40, 'own_half': 3, 'other_half': 3, 'assemble': 1, 'unpack_vectors': 1}
COUNT = [0]
MASKED = -1000000000.0
VMEM_LIMIT = 24 * 1024 * 1024
WIDE, NARROW = "wide", "narrow"
SMEM = pl.BlockSpec(memory_space=pltpu.SMEM)
VMEM = pl.BlockSpec(memory_space=pltpu.VMEM)
ANY = pl.BlockSpec(memory_space=pl.ANY)
VECTORS = (0, 1, 3, 5, 6, 7, 9, 11)
GAIN, SHIFT, LIFT, NUDGE, SCALE, CENTER, BOOST, SETTLE = range(8)


def like(shape, kind):
    return jax.ShapeDtypeStruct(tuple(shape), kind)


def fence(*items):
    fenced = lax.optimization_barrier(items)
    for old, new in zip(jax.tree.leaves(items), jax.tree.leaves(fenced)):
        if id(old) in ISSUED:
            ISSUED[id(new)] = new, ISSUED[id(old)][1]
    return fenced


ISSUED = {}


def launch(
    body, operands, out_shape, after=(), in_specs=None, out_specs=None, cover=SMALL,
    limit=VMEM_LIMIT, **more
):
    micros = COVERS.get(COUNT[0], COSTS.get(more["name"], cover))
    COUNT[0] += 1
    operands = list(operands)
    several = isinstance(out_shape, (list, tuple))
    outs = list(out_shape) if several else [out_shape]
    if in_specs is None:
        in_specs = [VMEM] * len(operands)
    if out_specs is None:
        out_specs = [VMEM] * len(outs)
    elif not isinstance(out_specs, (list, tuple)):
        out_specs = [out_specs]
    waits, specs = [], []
    for item in jax.tree.leaves(after):
        small = ISSUED.get(id(item))
        small = (item, ANY) if small is None else (small[1], VMEM)
        if all(small[0] is not w for w in waits):
            waits.append(small[0])
            specs.append(small[1])
    count = len(operands)
    first = count + len(waits)
    grid = "grid" in more

    def kernel(*refs):
        end = first + len(outs)
        refs[end][...] = jnp.zeros_like(refs[end])
        body(*refs[:count], *refs[first:end], *refs[end + 1 :])

    signal = like((8, LANES), F32)
    whole = pl.BlockSpec((8, LANES), lambda j: (0, 0)) if grid else VMEM
    if grid:
        specs = [whole if s is VMEM else s for s in specs]
    results = pl.pallas_call(
        kernel,
        out_shape=(*outs, signal),
        in_specs=[*in_specs, *specs],
        out_specs=(*out_specs, whole),
        compiler_params=pltpu.CompilerParams(vmem_limit_bytes=limit),
        cost_estimate=pl.CostEstimate(
            flops=int(micros * 1e9), bytes_accessed=1000, transcendentals=0
        ),
        **more,
    )(*operands, *waits)
    for item in results[:-1]:
        ISSUED[id(item)] = item, results[-1]
    return results[:-1] if several else results[0]


def dot(left, right):
    return lax.dot_general(left, right, (((1,), (0,)), ((), ())), preferred_element_type=F32)


def dot_nt(left, right):
    return lax.dot_general(left, right, (((1,), (1,)), ((), ())), preferred_element_type=F32)


def dot_tn(left, right):
    return lax.dot_general(left, right, (((0,), (0,)), ((), ())), preferred_element_type=F32)


def tables(segments, head_size):
    length = segments.shape[-1]
    before = jnp.sum((segments[:, None, :] < segments[:, :, None]).astype(jnp.int32), -1)
    place = jnp.arange(length, dtype=jnp.int32)
    position = (place[None, :] - before).astype(F32).reshape(-1, 1)
    half = ROT // 2
    lane = jnp.arange(LANES, dtype=jnp.int32) % head_size
    freqs = 10000.0 ** (-((lane % half).astype(F32) * 2.0 / ROT))
    angle = position * freqs[None, :]
    lane = lane[None, :]
    cosine = jnp.where(lane < ROT, jnp.cos(angle), 1.0)
    sine = jnp.sin(angle)
    low = jnp.where(lane < half, -sine, 0.0)
    high = jnp.where((lane >= half) & (lane < ROT), sine, 0.0)
    allowed = (segments[:, :, None] == segments[:, None, :]) & (place[:, None] <= place[None, :])[
        None
    ]
    return jnp.stack([cosine, low, high]), jnp.where(allowed, 0.0, -1.0).astype(F32)


def whiten(x):
    centered = x - jnp.mean(x, -1, keepdims=True)
    spread = jnp.mean(centered * centered, -1, keepdims=True)
    scale = lax.rsqrt(spread + EPS)
    return centered * scale, scale


def vector(vec_ref, layer, which, cols):
    at = layer * 8 + which
    return vec_ref[at : at + 1, cols]


def lane_masks(head_size, value):
    lane = lax.broadcasted_iota(jnp.int32, (1, LANES), 1)
    return [
        jnp.where((lane >= i * head_size) & (lane < (i + 1) * head_size), value, 0.0).astype(BF16)
        for i in range(LANES // head_size)
    ]


def stacked(block, masks):
    return jnp.concatenate([block * m for m in masks], 0)


def softmax_halves(scores, masked):
    out = []
    for i in range(scores.shape[0] // LANES):
        logits = jnp.where(masked, MASKED, scores[i * LANES : (i + 1) * LANES])
        expo = jnp.exp(logits - jnp.max(logits, 0, keepdims=True))
        out.append(expo * (1.0 / jnp.sum(expo, 0, keepdims=True)))
    return out


def norm_rows(h_ref, vec_ref, layer, which, out_ref, out_t_ref):
    tokens, width = h_ref.shape
    cols = slice(0, width)

    @pl.loop(0, tokens // LANES)
    def _(r):
        at = pl.ds(pl.multiple_of(r * LANES, LANES), LANES)
        normed, _ = whiten(h_ref[at, :].astype(F32))
        item = normed * vector(vec_ref, layer, which, cols)
        item = (item + vector(vec_ref, layer, which + 1, cols)).astype(BF16)
        out_ref[at, :] = item
        out_t_ref[:, at] = item.T


def run_attention_forward(layer, h, vec, packed, blend, turns, mask, after=()):
    tokens, width = h.shape
    head_size = width // HEADS
    rows, length, _ = mask.shape

    def body(
        h_ref, vec_ref, packed_ref, blend_ref, turn_ref, mask_ref,
        first_t_ref, q_ref, k_ref, v_ref, att_t_ref, base_ref,
        first_ref, att_ref,
    ):
        norm_rows(h_ref, vec_ref, layer, GAIN, first_ref, first_t_ref)
        tile = 2 * LANES
        for j in range(width // tile):
            for part, out_ref in enumerate((q_ref, k_ref, v_ref)):
                cols = slice(part * width + j * tile, part * width + (j + 1) * tile)
                mixed = dot(first_ref[...], packed_ref[:, cols])
                mixed = mixed + vector(vec_ref, layer, LIFT, cols)
                for b in range(tile // LANES):
                    block = mixed[:, b * LANES : (b + 1) * LANES]
                    if part < 2:
                        block = (
                            block * turn_ref[0]
                            + pltpu.roll(block, LANES - ROT // 2, 1) * turn_ref[1]
                            + pltpu.roll(block, ROT // 2, 1) * turn_ref[2]
                        )
                    start = j * tile + b * LANES
                    out_ref[:, start : start + LANES] = block.astype(BF16)

        scaled = lane_masks(head_size, head_size ** (-0.5))
        plain = lane_masks(head_size, 1.0)

        @pl.loop(0, rows)
        def _(r):
            at = pl.ds(pl.multiple_of(r * length, length), length)
            masked = mask_ref[r] < 0.0
            for p in range(width // LANES):
                cols = slice(p * LANES, (p + 1) * LANES)
                scores = dot_nt(stacked(k_ref[at, cols], scaled), q_ref[at, cols])
                probs = [p.astype(BF16) for p in softmax_halves(scores, masked)]
                probs = jnp.concatenate(probs, 0)
                attended = dot_tn(probs, stacked(v_ref[at, cols], plain)).astype(BF16)
                att_ref[at, cols] = attended
                att_t_ref[cols, at] = attended.T

        for j in range(width // tile):
            cols = slice(j * tile, (j + 1) * tile)
            base_ref[:, cols] = (
                h_ref[:, cols].astype(F32)
                + dot(att_ref[...], blend_ref[:, cols])
                + vector(vec_ref, layer, NUDGE, cols)
            )

    square = like((tokens, width), BF16)
    turned = like((width, tokens), BF16)
    return launch(
        body,
        (h, vec, packed, blend, turns, mask),
        (turned, square, square, square, turned, like((tokens, width), F32)),
        after,
        scratch_shapes=[pltpu.VMEM((tokens, width), BF16)] * 2,
        cover=COVER,
        name="attention_forward",
    )


def gelu_pair(u):
    z = jnp.abs(u) * 0.7071067811865476
    t = 1.0 / (1.0 + 0.3275911 * z)
    poly = t * (
        0.127414796
        + t * (-0.142248368 + t * (0.7107068705 + t * (-0.7265760135 + t * 0.5307027145)))
    )
    bell = jnp.exp(-0.5 * u * u)
    tail = poly * bell
    cdf = jnp.where(u < 0.0, tail, 1.0 - tail)
    return u * cdf, cdf + u * bell * 0.3989422804014327


def run_mlp_up(layer, h, vec, widen, after=(), tile=768):
    tokens, width = h.shape
    hidden = widen.shape[1]

    def body(h_ref, vec_ref, widen_ref, second_t_ref, active_t_ref, slope_ref, second_ref):
        step = pl.program_id(0)

        @pl.when(step == 0)
        def _():
            norm_rows(h_ref, vec_ref, layer, SCALE, second_ref, second_t_ref)

        cols = pl.ds(pl.multiple_of(step * tile, tile), tile)
        upward = dot(second_ref[...], widen_ref[...]) + vector(vec_ref, layer, BOOST, cols)
        active, slope = gelu_pair(upward)
        slope_ref[...] = slope.astype(BF16)
        active_t_ref[...] = active.astype(BF16).T

    whole = lambda shape: pl.BlockSpec(shape, lambda j: (0, 0))
    return launch(
        body,
        (h, vec, widen),
        (like((width, tokens), BF16), like((hidden, tokens), BF16), like((tokens, hidden), BF16)),
        after,
        grid=(hidden // tile,),
        in_specs=[
            whole((tokens, width)),
            whole(vec.shape),
            pl.BlockSpec((width, tile), lambda j: (0, j)),
        ],
        out_specs=(
            whole((width, tokens)),
            pl.BlockSpec((tile, tokens), lambda j: (j, 0)),
            pl.BlockSpec((tokens, tile), lambda j: (0, j)),
        ),
        scratch_shapes=[pltpu.VMEM((tokens, width), BF16)],
        cover=COVER,
        name="mlp_up",
    )


def run_mlp_down(layer, active_t, shrink, vec, base, kind, after=()):
    def body(active_t_ref, shrink_ref, vec_ref, base_ref, out_ref):
        tile = 2 * LANES
        for j in range(out_ref.shape[1] // tile):
            cols = slice(j * tile, (j + 1) * tile)
            total = dot_tn(active_t_ref[...], shrink_ref[:, cols])
            total = total + vector(vec_ref, layer, SETTLE, cols)
            out_ref[:, cols] = (base_ref[:, cols] + total).astype(out_ref.dtype)

    return launch(
        body, (active_t, shrink, vec, base), like(base.shape, kind), after, cover=COVER, name="mlp_down"
    )


def run_mlp_backward(grad, shrink, widen, slope, after=(), tile=1024):
    tokens, width = grad.shape
    hidden = widen.shape[1]

    def body(grad_ref, shrink_ref, widen_ref, slope_ref, up_ref, boost_ref, second_ref):
        step = pl.program_id(0)
        active = dot_nt(grad_ref[...], shrink_ref[...])
        up = (active * slope_ref[...].astype(F32)).astype(BF16)
        up_ref[...] = up
        boost_ref[...] = jnp.sum(up.astype(F32), 0, keepdims=True)
        back = dot_nt(up, widen_ref[...])

        @pl.when(step == 0)
        def _():
            second_ref[...] = back

        @pl.when(step > 0)
        def _():
            second_ref[...] += back

    whole = lambda shape: pl.BlockSpec(shape, lambda j: (0, 0))
    return launch(
        body,
        (grad, shrink, widen, slope),
        (like((tokens, hidden), BF16), like((1, hidden), F32), like((tokens, width), F32)),
        after,
        grid=(hidden // tile,),
        in_specs=[
            whole((tokens, width)),
            pl.BlockSpec((tile, width), lambda j: (j, 0)),
            pl.BlockSpec((width, tile), lambda j: (0, j)),
            pl.BlockSpec((tokens, tile), lambda j: (0, j)),
        ],
        out_specs=(
            pl.BlockSpec((tokens, tile), lambda j: (0, j)),
            pl.BlockSpec((1, tile), lambda j: (0, j)),
            whole((tokens, width)),
        ),
        cover=COVER,
        name="mlp_backward",
    )


def run_attention_backward(grad, blend, q, k, v, turns, mask, after=()):
    tokens, width = grad.shape
    head_size = width // HEADS
    rows, length, _ = mask.shape

    def body(
        grad_ref, blend_ref, q_ref, k_ref, v_ref, turn_ref, mask_ref, mixed_ref, lift_ref, datt_ref
    ):
        tile = 2 * LANES
        for j in range(width // tile):
            cols = slice(j * tile, (j + 1) * tile)
            datt_ref[:, cols] = dot_nt(grad_ref[...], blend_ref[cols, :]).astype(BF16)

        scaled = lane_masks(head_size, head_size ** (-0.5))
        plain = lane_masks(head_size, 1.0)

        @pl.loop(0, rows)
        def _(r):
            at = pl.ds(pl.multiple_of(r * length, length), length)
            masked = mask_ref[r] < 0.0
            cos, low, high = turn_ref[0, at, :], turn_ref[1, at, :], turn_ref[2, at, :]

            def unturn(block):
                return (
                    block * cos
                    + pltpu.roll(block * low, ROT // 2, 1)
                    + pltpu.roll(block * high, LANES - ROT // 2, 1)
                )

            lane = lax.broadcasted_iota(jnp.int32, (length, LANES), 1)
            for p in range(width // LANES):
                cols = slice(p * LANES, (p + 1) * LANES)
                query, values, datt = q_ref[at, cols], v_ref[at, cols], datt_ref[at, cols]
                keys = stacked(k_ref[at, cols], scaled)
                probs = softmax_halves(dot_nt(keys, query), masked)
                dprobs = dot_nt(stacked(values, plain), datt)
                draw = []
                for i, prob in enumerate(probs):
                    dprob = dprobs[i * LANES : (i + 1) * LANES]
                    inner = jnp.sum(prob * dprob, 0, keepdims=True)
                    draw.append((prob * (dprob - inner)).astype(BF16))
                draw = jnp.concatenate(draw, 0)
                low_probs = jnp.concatenate([x.astype(BF16) for x in probs], 0)
                dvalues = dot(low_probs, datt)
                dkeys = dot(draw, query)
                dquery = dot_tn(draw, keys)
                dvalues = jnp.where(lane < head_size, dvalues[:length], dvalues[length:])
                dkeys = jnp.where(lane < head_size, dkeys[:length], dkeys[length:])
                dkeys = dkeys * (head_size ** (-0.5))
                for part, item in enumerate((unturn(dquery), unturn(dkeys), dvalues)):
                    start = part * width + p * LANES
                    mixed_ref[at, start : start + LANES] = item.astype(BF16)

        for j in range(3 * width // tile):
            cols = slice(j * tile, (j + 1) * tile)
            lift_ref[:, cols] = jnp.sum(mixed_ref[:, cols].astype(F32), 0, keepdims=True)

    return launch(
        body,
        (grad, blend, q, k, v, turns, mask),
        (like((tokens, 3 * width), BF16), like((1, 3 * width), F32)),
        after,
        scratch_shapes=[pltpu.VMEM((tokens, width), BF16)],
        cover=COVER,
        name="attention_backward",
    )


def run_stream_backward(layer, grad, out_grad, h, vec, second, packed, mixed, after=()):
    tokens, width = grad.shape

    def body(
        grad_ref, out_grad_ref, h_ref, vec_ref, second_ref, packed_ref, mixed_ref,
        in_grad_ref, low_ref, sums_ref,
        dfirst_ref,
    ):
        tile = 2 * LANES
        for j in range(width // tile):
            cols = slice(j * tile, (j + 1) * tile)
            dfirst_ref[:, cols] = dot_nt(mixed_ref[...], packed_ref[cols, :])
        sums_ref[...] = jnp.zeros_like(sums_ref)
        cols = slice(0, width)

        @pl.loop(0, tokens // LANES)
        def _(r):
            at = pl.ds(pl.multiple_of(r * LANES, LANES), LANES)
            normed, spread = whiten(h_ref[at, :].astype(F32))
            first, second = dfirst_ref[at, :], second_ref[at, :]
            low_grad = grad_ref[at, :].astype(F32)
            for i, item in enumerate((first * normed, first, second * normed, second, low_grad)):
                sums_ref[i : i + 1, :] += jnp.sum(item, 0, keepdims=True)
            inner = first * vector(vec_ref, layer, GAIN, cols)
            inner = inner + second * vector(vec_ref, layer, SCALE, cols)
            along = jnp.mean(inner * normed, -1, keepdims=True)
            inner = inner - jnp.mean(inner, -1, keepdims=True) - normed * along
            total = out_grad_ref[at, :].astype(F32) + inner * spread
            in_grad_ref[at, :] = total
            low_ref[at, :] = total.astype(BF16)

    return launch(
        body,
        (grad, out_grad, h, vec, second, packed, mixed),
        (like((tokens, width), F32), like((tokens, width), BF16), like((8, width), F32)),
        after,
        scratch_shapes=[pltpu.VMEM((tokens, width), F32)],
        cover=COVER,
        name="stream_backward",
    )


def sizes(unit):
    return (unit, unit, 3 * unit, unit, unit, unit, 4 * unit, unit)


def row(item):
    return item.reshape(1, -1)


def owner_masks(devices, size):
    total = devices * size
    r = lax.broadcasted_iota(jnp.int32, (devices, total), 1)
    d = lax.broadcasted_iota(jnp.int32, (devices, total), 0) * size
    own = ((r >= d) & (r < d + size)).astype(F32)
    r = lax.broadcasted_iota(jnp.int32, (1, total), 1).astype(F32)
    r = r - jnp.floor((r + 0.5) * (1.0 / size)) * size
    lane = lax.broadcasted_iota(jnp.int32, (LANES, total), 0).astype(F32)
    return own, (lane == r).astype(BF16)


def unpack_vectors(block):
    devices, unit, _ = block.shape

    def body(v_ref, out_ref, held):
        held[...] = v_ref[...].astype(F32)
        for size in (unit, 3 * unit, 4 * unit):
            own, lane = owner_masks(devices, size)
            for i in range(16):
                if sizes(unit)[i % 8] == size:
                    item = dot(held[:, i, :].astype(BF16), lane)
                    out_ref[i : i + 1, : devices * size] = jnp.sum(own * item, 0, keepdims=True)

    return launch(
        body,
        (block,),
        like((16, 4 * devices * unit), F32),
        scratch_shapes=[pltpu.VMEM(block.shape, F32)],
        name="unpack_vectors",
    )


def pack_gradients(sums, lift, boost, devices, after=()):
    unit = sums.shape[1] // devices
    shape = (devices, unit, LANES)

    def body(sums_ref, lift_ref, boost_ref, out_ref, held):
        held[...] = jnp.zeros_like(held)
        items = zip((GAIN, SHIFT, SCALE, CENTER, SETTLE), range(5))
        items = [(i, sums_ref[r : r + 1, :]) for i, r in items]
        for size, parts in (
            (unit, items),
            (3 * unit, [(LIFT, lift_ref[...])]),
            (4 * unit, [(BOOST, boost_ref[...])]),
        ):
            own, lane = owner_masks(devices, size)
            for i, value in parts:
                held[:, i, :] = dot_nt((own * value).astype(BF16), lane)
        out_ref[...] = held[...].astype(BF16)

    return launch(
        body,
        (sums, lift, boost),
        like(shape, BF16),
        after,
        scratch_shapes=[pltpu.VMEM(shape, F32)],
        name="pack_gradients",
    )


def flip(item, bit):
    return lax.ppermute(item, WIDE, [(i, i ^ bit) for i in range(8)])


def across_core(item):
    return flip(item, 1)


def across_x(item):
    return flip(item, 2)


def across_y(item):
    return flip(item, 4)


def along_z(item, step):
    return lax.ppermute(item, NARROW, [(i, (i + step) % 4) for i in range(4)])


def pack_shares(layers, matrices, unit):
    items = [row(layer[i]) for layer in layers for i in VECTORS]
    width = sum(m.shape[1] for m in matrices)
    count = len(matrices) + len(items)

    def body(*refs):
        mats, ins = refs[: len(matrices)], refs[len(matrices) : count]
        out_ref, held, sem, *parts = refs[count:]
        at, copies = 0, []
        for m in mats:
            target = out_ref.at[:, pl.ds(at, m.shape[1])]
            copies.append(pltpu.make_async_copy(m, target, sem.at[len(copies)]))
            at += m.shape[1]
        for item, part in zip(ins, parts):
            copies.append(pltpu.make_async_copy(item, part, sem.at[len(copies)]))
        for copy in copies:
            copy.start()
        held[...] = jnp.zeros_like(held)
        for copy in copies:
            copy.wait()
        for i, part in enumerate(parts):
            held[i : i + 1, : part.shape[1]] = part[...].astype(F32)
        out_ref[:, at:] = held[...].astype(BF16)

    return launch(
        body,
        [*matrices, *items],
        like((unit, width + LANES), BF16),
        in_specs=[ANY] * count,
        scratch_shapes=[pltpu.VMEM((unit, LANES), F32), pltpu.SemaphoreType.DMA((count,))]
        + [pltpu.VMEM(i.shape, BF16) for i in items],
        limit=60 * 1024 * 1024,
        name="pack_shares",
    )


def beside(items, unit, after=(), cover=SMALL):
    width = sum(i.shape[0] // unit * i.shape[1] for i in items)

    def body(*refs):
        out_ref, at = refs[-1], 0
        for item in refs[:-1]:
            for q in range(item.shape[0] // unit):
                out_ref[:, at : at + item.shape[1]] = item[q * unit : (q + 1) * unit, :]
                at += item.shape[1]

    return launch(
        body, items, like((unit, width), BF16), after, cover=cover, name="beside"
    )


class Gather:

    def __init__(self, share, where, widths):
        self.share, self.where, self.widths = share, where, widths
        self.ring = [share] + [along_z(share, k) for k in (1, 2, 3)]

    def stack(self, after=()):
        z = self.where[2]
        slots = jnp.stack([(z - k) % 4 for k in range(4)]).astype(jnp.int32)
        unit = self.share.shape[0]

        def body(slot_ref, *refs):
            items, outs = refs[:4], refs[4:]
            for i, item in enumerate(items):
                start = 0
                for out, width in zip(outs, self.widths):
                    out[slot_ref[i]] = item[:, start : start + width]
                    start += width

        outs = launch(
            body,
            (slots, *self.ring),
            [like((4, unit, w), BF16) for w in self.widths],
            after,
            in_specs=[SMEM] + [VMEM] * 4,
            name="stack_ring",
        )
        return [Plane(o, self.where) for o in outs]


class Plane:

    def __init__(self, own, where):
        self.own, self.where = own, where

    def near(self):
        self.sides = across_x(self.own), across_y(self.own)
        return self.sides

    def cut(self, after=()):
        shape = like((2,) + self.own.shape[1:], BF16)

        def body(left_ref, up_ref, up_out, left_out):
            up_out[...] = up_ref[:2]
            left_out[...] = left_ref[2:]

        self.halves = launch(body, self.sides, (shape, shape), after, name="cut")
        self.mine = (self.own, *self.sides)
        return self.halves

    def corner(self):
        self.halves, self.mine = fence(self.halves, self.mine)
        up, left = self.halves
        self.far = across_x(up), across_y(left)
        self.other = tuple(across_core(m) for m in self.mine)
        return self.far

    def assemble(self, widths, folds, after=()):
        plane, core, _ = self.where
        pieces = (*self.mine, *self.far, *self.other, *(across_core(f) for f in self.far))
        slots = jnp.stack(
            [(plane ^ r) * 2 + c for c in (core, 1 - core) for r in range(4)]
        ).astype(jnp.int32)
        unit = self.own.shape[1]

        def body(slot_ref, *refs):
            items, outs = refs[:10], refs[10:]
            for i, piece in enumerate(items):
                side, i = divmod(i, 5)
                slot = slot_ref[side * 4 + min(i, 3)]
                first = 2 if i == 4 else 0
                for z in range(piece.shape[0]):
                    start = 0
                    for out, width, fold in zip(outs, widths, folds):
                        part = width // fold
                        for q in range(fold):
                            cols = slice(start + q * part, start + (q + 1) * part)
                            if fold > 1:
                                out[slot, first + z, q] = piece[z, :, cols]
                            else:
                                out[slot, first + z] = piece[z, :, cols]
                        start += width

        outs = launch(
            body,
            (slots, *pieces),
            [
                like((8, 4, f, unit, w // f) if f > 1 else (8, 4, unit, w), BF16)
                for w, f in zip(widths, folds)
            ],
            after,
            in_specs=[SMEM] + [VMEM] * 10,
            name="assemble",
        )
        return [o.reshape(-1, o.shape[-1]) for o in outs]


def half_kernel(folds, tile, own, extra):
    count = len(folds)

    def body(index_ref, *refs):
        lefts, rights, refs = refs[:count], refs[count : 2 * count], refs[2 * count :]
        if extra:
            extra_ref, refs = refs[0], refs[1:]
        if own:
            arrived, refs = refs[0], refs[1:]
        keeps, outs = refs[-count:], refs[:-count]

        def emit(total, cols):
            if not own:
                outs[0][:, :, :, cols] = total.astype(BF16)
                return
            total = (total.astype(F32) + arrived[:, :, :, cols].astype(F32)).astype(BF16)
            p_ref, x_ref, y_ref, xp_ref, yp_ref = outs
            p_ref[:, :, cols] = total[0]
            x_ref[0, :, :, cols] = total[3, :2]
            x_ref[1, :, :, cols] = total[1, :2]
            xp_ref[:, :, cols] = total[1, 2:]
            y_ref[0, :, :, cols] = total[3, 2:]
            y_ref[1, :, :, cols] = total[2, 2:]
            yp_ref[:, :, cols] = total[2, :2]

        start = 0
        for left, right, keep, fold in zip(lefts, rights, keeps, folds):
            size = left.shape[0] // 8
            for r in range(4):
                at = pl.ds(pl.multiple_of(index_ref[r] * size, size), size)
                keep[r * size : (r + 1) * size, :] = left[at, :]
            width = right.shape[1]
            for j in range(0, width, tile):
                total = dot(keep[...], right[:, j : j + tile])
                total = total.reshape(4, 4, fold, size // 4 // fold, tile)
                for q in range(fold):
                    at = start + q * width + j
                    emit(total[:, :, q], slice(at, at + tile))
            start += fold * width
        if extra:
            total = jnp.stack([extra_ref[index_ref[r]] for r in range(4)])
            emit(total, slice(start, start + LANES))

    return body


class Scatter:

    def __init__(self, terms, extra, where):
        self.terms, self.extra, self.where = terms, extra, where
        self.unit = terms[0][0].shape[0] // 32 // terms[0][2]
        self.columns = sum(r.shape[1] * f for _, r, f in terms)
        self.columns += 0 if extra is None else LANES

    def half(self, core, arrived, after, tile=256):
        plane = self.where[0]
        index = jnp.stack([(plane ^ r) * 2 + core for r in range(4)]).astype(jnp.int32)
        lefts, rights, folds = zip(*self.terms)
        own = arrived is not None
        block = lambda *shape: like(shape + (self.unit, self.columns), BF16)
        if own:
            shapes = (block(4), block(2, 2), block(2, 2), block(2), block(2))
        else:
            shapes = block(4, 4)
        operands = [index, *lefts, *rights]
        if self.extra is not None:
            operands.append(self.extra.reshape(8, 4, self.unit, LANES))
        if own:
            operands.append(arrived)
        return launch(
            half_kernel(folds, tile, own, self.extra is not None),
            operands,
            shapes,
            after,
            in_specs=[SMEM] + [VMEM] * (len(operands) - 1),
            scratch_shapes=[pltpu.VMEM((l.shape[0] // 2, l.shape[1]), BF16) for l in lefts],
            name="own_half" if own else "other_half",
        )

    def other(self, after=()):
        out = self.half(1 - self.where[1], None, after)
        self.arrived = across_core(out)
        return out

    def own(self, after=()):
        self.p, x, y, self.xp, self.yp = self.half(self.where[1], self.arrived, after)
        self.x1, self.y1 = across_x(x), across_y(y)
        return self.p

    def far(self, after=()):
        shape = like(self.xp.shape, BF16)

        def body(xp_ref, y1_ref, yp_ref, x1_ref, x_ref, y_ref):
            x_ref[...] = (xp_ref[...].astype(F32) + y1_ref[0].astype(F32)).astype(BF16)
            y_ref[...] = (yp_ref[...].astype(F32) + x1_ref[0].astype(F32)).astype(BF16)

        operands = (self.xp, self.y1, self.yp, self.x1)
        xs, ys = launch(body, operands, (shape, shape), after, name="add_far")
        self.x2, self.y2 = across_x(xs), across_y(ys)
        return xs

    def near(self):
        return self.p, self.x1, self.y2, self.y1, self.x2


class Ring:

    def __init__(self, scatters):
        self.scatters = scatters
        self.unit = scatters[0].unit
        self.columns = sum(s.columns for s in scatters)

    def join(self, after=()):
        z = self.scatters[0].where[2]
        turn = jnp.stack([(z + k) % 4 for k in range(4)]).astype(jnp.int32)
        operands = [o for s in self.scatters for o in s.near()]
        widths = [s.columns for s in self.scatters]

        def body(turn_ref, *refs):
            ins, outs, held = refs[: len(operands)], refs[len(operands) : -1], refs[-1]
            start = 0
            for i, width in enumerate(widths):
                p_ref, x1_ref, y2_ref, y1_ref, x2_ref = ins[5 * i : 5 * i + 5]
                cols = slice(start, start + width)
                held[0:2, :, cols] = (
                    p_ref[0:2].astype(F32) + x1_ref[1].astype(F32) + y2_ref[...].astype(F32)
                )
                held[2:4, :, cols] = (
                    p_ref[2:4].astype(F32) + y1_ref[1].astype(F32) + x2_ref[...].astype(F32)
                )
                start += width
            for k, out in enumerate(outs):
                out[...] = held[turn_ref[k]].astype(BF16)

        blocks = launch(
            body,
            (turn, *operands),
            [like((self.unit, self.columns), BF16)] * 4,
            after,
            in_specs=[SMEM] + [VMEM] * len(operands),
            scratch_shapes=[pltpu.VMEM((4, self.unit, self.columns), F32)],
            name="join_plane",
        )
        self.got = [blocks[0]] + [along_z(blocks[k], k) for k in (1, 2, 3)]
        return blocks[0]

    def finish(self, widths, folds, vectors, after=(), cover=SMALL):
        unit = self.unit
        shapes = [like((f * unit, w), F32) for w, f in zip(widths, folds)]
        if vectors:
            shapes += [like((1, n), F32) for n in sizes(unit)]

        def body(*refs):
            ins, outs = refs[:4], refs[4:]

            def total(cols):
                return (
                    ins[0][:, cols].astype(F32)
                    + ins[1][:, cols].astype(F32)
                    + ins[2][:, cols].astype(F32)
                    + ins[3][:, cols].astype(F32)
                )

            start = 0
            for out, width, fold in zip(outs, widths, folds):
                for q in range(fold):
                    out[q * unit : (q + 1) * unit, :] = total(slice(start, start + width))
                    start += width
            if vectors:
                block = total(slice(start, start + LANES))
                for i, (out, n) in enumerate(zip(outs[len(widths) :], sizes(unit))):
                    out[...] = block[i : i + 1, :n]

        return launch(body, self.got, shapes, after, cover=cover, name="sum_ring")


def on_cube(stream, cotangent, segment_ids, *weights):
    one, two = weights[:12], weights[12:]
    unit = one[0].shape[0]
    count, length, width = stream.shape
    tokens = count * length
    hidden = 4 * width
    wide = lax.axis_index(WIDE)
    where = (wide // 2, wide % 2, lax.axis_index(NARROW))
    three = 3 * width
    h = stream.reshape(tokens, width)

    ISSUED.clear()
    COUNT[0] = 0
    head_share = pack_shares((one, two), [one[2], one[4]], unit)
    z_head = Gather(head_share, where, [4 * width + LANES])
    tail_share = beside([one[8], one[10]], unit, head_share)
    z_tail = Gather(tail_share, where, [2 * hidden])
    turns, mask = tables(segment_ids, width // HEADS)
    (h1,) = z_head.stack((turns, mask))
    near = h1.near()
    head_two = beside([two[2], two[4]], unit, (tail_share, h1.own))
    tail_two = beside([two[8], two[10]], unit, head_two)
    h1.cut((tail_two, z_tail.ring[1:]))
    (t1,) = z_tail.stack(h1.halves)
    h1.halves, t1.own, head_two = fence(h1.halves, t1.own, head_two)
    corner = h1.corner()
    near = t1.near()
    z_two = Gather(head_two, where, [4 * width])
    packed, blend, block = h1.assemble((three, width, LANES), (1, 1, 1))
    vec = unpack_vectors(block.reshape(32, unit, LANES))
    first_t, q, k, v, att_t, base = run_attention_forward(0, h, vec, packed, blend, turns, mask)
    t1.cut((base, z_two.ring[1:]))
    (h2,) = z_two.stack(t1.halves)
    t1.halves, h2.own, tail_two = fence(t1.halves, h2.own, tail_two)
    corner = t1.corner()
    near = h2.near()
    z_last = Gather(tail_two, where, [hidden, hidden])
    widen, shrink = t1.assemble((hidden, hidden), (1, 4))
    second_t, active_t, slope = run_mlp_up(0, h, vec, widen)
    h2.cut(active_t)
    middle = run_mlp_down(0, active_t, shrink, vec, base, F32)
    saved = h, first_t, q, k, v, att_t, second_t, active_t, slope, packed, blend, widen, shrink
    w2, s2 = z_last.stack((h2.halves, middle))
    corner = h2.corner()
    near = w2.near()
    packed, blend = h2.assemble((three, width), (1, 1))
    first_t, q, k, v, att_t, base = run_attention_forward(
        1, middle, vec, packed, blend, turns, mask
    )
    w2.cut(base)
    w2.halves, s2.own = fence(w2.halves, s2.own)
    corner = w2.corner()
    near = s2.near()
    (widen,) = w2.assemble((hidden,), (1,))
    second_t, active_t, slope = run_mlp_up(1, middle, vec, widen)
    grad = low = cotangent.reshape(tokens, width)
    gs2 = Scatter([(active_t, low, 4)], None, where)
    token = gs2.other(active_t)
    s2.cut(token)
    s2.corner()
    token = gs2.own(token)
    (shrink,) = s2.assemble((hidden,), (4,), token)

    up, g_boost, back = run_mlp_backward(low, shrink, widen, slope)
    gw2 = Scatter([(second_t, up, 1)], None, where)
    token = gw2.other(back)
    token = gs2.far((token, gs2.x1, gs2.y1))
    mixed, g_lift = run_attention_backward(low, blend, q, k, v, turns, mask, token)
    token = gw2.own((mixed, gs2.x2, gs2.y2))
    grad, low_one, sums = run_stream_backward(
        1, low, grad, middle, vec, back, packed, mixed, token
    )
    extra = pack_gradients(sums, g_lift, g_boost, 32)
    last = active_t, shrink, vec, base
    h, first_one, q, k, v, att_one, second_t, active_t, slope, packed, blend, widen, shrink = saved
    gp2 = Scatter([(first_t, mixed, 1), (att_t, low, 1)], extra, where)
    token = gp2.other(extra)
    token = gw2.far(token)
    low = low_one
    up, g_boost, back = run_mlp_backward(low, shrink, widen, slope, token)
    gm1 = Scatter([(active_t, low, 4), (second_t, up, 1)], None, where)
    token = gp2.own((back, gw2.x2, gw2.y2))
    token = gm1.other(token)
    ring_two = Ring([gs2, gw2])
    token = ring_two.join(token)
    mixed, g_lift = run_attention_backward(low, blend, q, k, v, turns, mask, token)
    token = gp2.far(mixed)
    token = gm1.own(token)
    s_two, w_two = ring_two.finish((width, hidden), (4, 1), False, token)
    token = s_two
    grad, _, sums = run_stream_backward(0, low, grad, h, vec, back, packed, mixed, token)
    extra = pack_gradients(sums, g_lift, g_boost, 32)
    gp1 = Scatter([(first_one, mixed, 1), (att_one, low, 1)], extra, where)
    token = gp1.other(extra)
    ring_two_p, ring_one, ring_end = Ring([gp2]), Ring([gm1]), Ring([gp1])
    token = ring_two_p.join(token)
    token = gp1.own(token)
    token = gm1.far(token)
    token = ending = run_mlp_down(1, *last, BF16, token)
    p_two, b_two, *v_two = ring_two_p.finish((three, width), (1, 1), True, token)
    token = gp1.far(p_two)
    token = ring_one.join(token)
    token = ring_end.join(token)
    s_one, w_one = ring_one.finish((width, hidden), (4, 1), False, token)
    p_one, b_one, *v_one = ring_end.finish((three, width), (1, 1), True, w_one)

    out = []
    for p, b, w, s, v in (
        (p_one, b_one, w_one, s_one, v_one),
        (p_two, b_two, w_two, s_two, v_two),
    ):
        g = [None] * 12
        g[2], g[4], g[8], g[10] = p, b, w, s
        for i, item in zip(VECTORS, v):
            g[i] = item.reshape(-1)
        g[5] = g[11]
        out += g
    shape = (count, length, width)
    return (ending.reshape(shape), grad.reshape(shape)) + tuple(out)


def whole(item):
    return lax.all_gather(item, (WIDE, NARROW), axis=0, tiled=True)


def owned(item):
    for axis in (WIDE, NARROW):
        parts = lax.axis_size(axis)
        item = item.reshape((parts, item.shape[0] // parts) + item.shape[1:])
        item = lax.all_to_all(item.astype(BF16), axis, 0, 0, tiled=True)
        item = jnp.sum(item.astype(F32), 0)
    return item


def on_any(stream, cotangent, segment_ids, *weights):
    count, length, width = stream.shape
    tokens = count * length
    turns, mask = tables(segment_ids, width // HEADS)
    layers = [[whole(i) for i in layer] for layer in (weights[:12], weights[12:])]
    hidden = layers[0][9].shape[0]
    vec = [row(w[i]).astype(F32) for w in layers for i in VECTORS]
    vec = jnp.concatenate([jnp.pad(i, ((0, 0), (0, hidden - i.shape[1]))) for i in vec])
    h = stream.reshape(tokens, width)
    kept = []
    for l, w in enumerate(layers):
        packed, blend, widen, shrink = w[2], w[4], w[8], w[10]
        first_t, q, k, v, att_t, base = run_attention_forward(
            l, h, vec, packed, blend, turns, mask
        )
        second_t, active_t, slope = run_mlp_up(l, h, vec, widen)
        out = run_mlp_down(l, active_t, shrink, vec, base, F32)
        kept.append((h, first_t, q, k, v, att_t, second_t, active_t, slope))
        h = out
    result = h.astype(BF16).reshape(stream.shape)
    grad = low = cotangent.reshape(tokens, width)
    out = ()
    for l in (1, 0):
        h, first_t, q, k, v, att_t, second_t, active_t, slope = kept[l]
        packed, blend, widen, shrink = (layers[l][i] for i in (2, 4, 8, 10))
        up, g_boost, back = run_mlp_backward(low, shrink, widen, slope)
        mixed, g_lift = run_attention_backward(low, blend, q, k, v, turns, mask)
        grad, next_low, sums = run_stream_backward(l, low, grad, h, vec, back, packed, mixed)
        g_gain, g_shift, g_scale, g_center, g_settle = (owned(sums[i]) for i in range(5))
        out = (
            g_gain,
            g_shift,
            owned(dot(first_t, mixed)),
            owned(g_lift[0]),
            owned(dot(att_t, low)),
            g_settle,
            g_scale,
            g_center,
            owned(dot(second_t, up)),
            owned(g_boost[0]),
            owned(dot(active_t, low)),
            g_settle,
        ) + out
        low = next_low
    return (result, grad.reshape(stream.shape)) + out


def solution(mesh):
    axes = (WIDE, NARROW)
    one, two, three = P(axes), P(axes, None), P(axes, None, None)
    layer = (one, one, two, one, two, one, one, one, two, one, two, one)
    cube = dict(mesh.shape) == {WIDE: 8, NARROW: 4}
    return jax.shard_map(
        on_cube if cube else on_any,
        mesh=mesh,
        in_specs=(three, three, two) + layer + layer,
        out_specs=(three, three) + layer + layer,
        check_vma=False,
    )
```
